256 devices in a mesh: step: 16 (over x, y), seq: 16 (over z, core).
Axes of the slice: x: 4, y: 4, z: 8, core: 2. Of those that a mesh axis runs over, the one named last changes fastest.
Arguments:
- states: float32 [16, 4096, 1280], P('step', 'seq'), may hold values from -6 to 6
- start: float32 [4096, 1280], P('seq'), may hold values from -6 to 6
- noise: bfloat16 [16, 4096, 1280], P('step', 'seq'), may hold values from -6 to 6
- coefficients: float32 [16, 3], P('step'), may hold values from 0.05 to 0.4
- context: bfloat16 [16, 4096, 1024], P('step', None, 'seq'), may hold values from -6 to 6
- qkv_weight: bfloat16 [1280, 3072], P('step'), may hold values from -5 to 5, as said below
- out_weights: bfloat16 [2, 1024, 1280], P(None, 'step'), may hold values from -0.1875 to 0.1875
- gain: float32 [1280], replicated, may hold values from 0.5 to 1.5
Outputs:
- advanced: float32 [16, 4096, 1280], P('step', 'seq')
- mixed: float32 [16, 4096, 1280], P('step', 'seq')
The draws below stay inside these ranges and needn't reach their ends.
Inputs may be any that keep to these rules, and one draw needn't show every extreme that they name: `qkv_weight`: entries within 40 / sqrt(1280) in magnitude.
All inputs are finite; a program needn't handle non-finite values.
Results may differ from the reference program's by a relative error of at most 0.002.
Values may be sent and summed in bfloat16 or wider, within the bound.
No kernel may reach another device: no remote copies, remote signals or barrier semaphores. Data moves between devices by JAX's collectives and lax.ppermute only.
A program may use at most 128 MiB of HBM per device.

```python
import math
import jax
import jax.numpy as jnp
from jax import lax

D = 1280
HEADS = 16
HEAD_DIM = 64
INNER = 1024
TOKENS = 4096
STEPS = 16


def draw_qkv_weight(key, part):
    key = jax.random.fold_in(key, 11)
    first = jax.random.fold_in(key, 0)
    normal_part = jnp.clip(jax.random.normal(first, (D, 3, HEADS, HEAD_DIM), jnp.float32), -6.0, 6.0)
    base = normal_part / math.sqrt(D)
    return base.reshape(D, 3 * HEADS * HEAD_DIM).astype(jnp.bfloat16)


def steps_of(key, extent, pieces, low, top_value):
    loudness = 1.0
    for position, blocks in pieces:
        heights = jax.random.uniform(jax.random.fold_in(jax.random.fold_in(key, 6), position), (blocks,), jnp.float32, low / len(pieces), top_value / len(pieces))
        loudness = loudness * jnp.repeat(jnp.exp(heights), extent[position] // blocks).reshape((-1,) + (1,) * (len(extent) - 1 - position))
    return loudness


def gaussian(rng, dims, width, most, cuts=(), kind=jnp.bfloat16):
    drawn = jax.random.normal(rng, dims, jnp.float32) * width
    if len(cuts) > 0:
        drawn = steps_of(rng, dims, cuts, -0.22, 0.18) * drawn
    return jnp.clip(drawn, min=-most, max=most).astype(kind)


def setup_inputs(seed: int = 0) -> dict:
    key_list = jax.random.split(jax.random.key(seed), 9)
    return {
        "states": gaussian(key_list[0], (STEPS, TOKENS, D), 1.0, 6.0, ((0, 16), (1, 16)), jnp.float32),
        "start": gaussian(key_list[1], (TOKENS, D), 1.0, 6.0, ((0, 16),), jnp.float32),
        "noise": gaussian(key_list[2], (STEPS, TOKENS, D), 1.0, 6.0, ((0, 16), (1, 16))),
        "coefficients": jnp.clip(0.05 + 0.35 * jax.random.uniform(key_list[3], (STEPS, 3), jnp.float32) ** steps_of(key_list[3], (STEPS, 3), ((0, 16),), -0.2, 0.2), 0.05, 0.4),
        "context": gaussian(key_list[4], (STEPS, TOKENS, INNER), 1.0, 6.0, ((0, 16), (2, 16))),
        "qkv_weight": draw_qkv_weight(jax.random.fold_in(key_list[8], 71), 0),
        "out_weights": gaussian(key_list[6], (2, INNER, D), INNER ** -0.5, 0.1875, ((1, 16),)),
        "gain": jnp.clip(1.0 + 0.1 * jax.random.normal(key_list[7], (D,), jnp.float32), 0.5, 1.5),
    }


def layer_norm(rows, gain):
    mean = lax.optimization_barrier(jnp.mean(rows, axis=-1, keepdims=True))
    centred = rows - mean
    variance = lax.optimization_barrier(jnp.mean(centred * centred, axis=-1, keepdims=True))
    return (centred * lax.rsqrt(variance + 1e-05) * gain).astype(jnp.bfloat16)

def attention(qkv):
    split = qkv.reshape(TOKENS, 3, HEADS, HEAD_DIM).transpose(2, 1, 0, 3)
    scale = 1.0 / math.sqrt(HEAD_DIM)

    def head(item):
        scores = jnp.dot(item[0], item[1].T, preferred_element_type=jnp.float32) * scale
        top = lax.optimization_barrier(jnp.max(scores, axis=-1, keepdims=True))
        weights = jnp.exp(scores - top)
        weights = (weights / lax.optimization_barrier(jnp.sum(weights, axis=-1, keepdims=True))).astype(jnp.bfloat16)
        return jnp.dot(weights, item[2], preferred_element_type=jnp.float32).astype(jnp.bfloat16)
    result = lax.map(head, split)
    return result.transpose(1, 0, 2).reshape(TOKENS, INNER)

def reference(states, start, noise, coefficients, context, qkv_weight, out_weights, gain):

    def drift_of(item):
        state_rows, noise_rows, factors, heads_rows = item
        features = state_rows + jnp.dot(heads_rows, out_weights[0], preferred_element_type=jnp.float32)
        return factors[0] * state_rows + factors[1] * features + factors[2] * noise_rows.astype(jnp.float32)
    drift = lax.map(drift_of, (states, noise, coefficients, context))
    running = jnp.cumsum(drift, axis=0)
    prefix = jnp.concatenate([jnp.zeros((1, TOKENS, D), jnp.float32), running[:-1]], axis=0)
    advanced = start[None] + prefix

    def layer(rows):
        normed = layer_norm(rows, gain)
        qkv = jnp.dot(normed, qkv_weight, preferred_element_type=jnp.float32).astype(jnp.bfloat16)
        attended = attention(qkv)
        return rows + jnp.dot(attended, out_weights[1], preferred_element_type=jnp.float32)
    mixed = lax.map(layer, advanced)
    return (advanced, mixed)
```

```python
import jax
import jax.numpy as jnp
from jax import lax
from jax.experimental import pallas as pl
from jax.experimental.pallas import tpu as pltpu
from jax.sharding import PartitionSpec as P

HEAD_DIM = 64


def attention_kernel(qkv_ref, out_ref, value_rows, scores):
    block = pl.program_id(0)
    blocks, _, dim, rows = qkv_ref.shape

    @pl.when(block == 0)
    def _():
        for j in range(blocks):
            values = qkv_ref[j, 2].astype(jnp.float32)
            padded = jnp.concatenate([values, jnp.ones((dim, rows), jnp.float32)], axis=0)
            value_rows[j * rows : (j + 1) * rows, :] = padded.T.astype(jnp.bfloat16)

    query = qkv_ref[block, 0].astype(jnp.float32) * (HEAD_DIM**-0.5)
    query = jnp.concatenate([query, query], axis=0).T[:, :dim].astype(jnp.bfloat16)
    top = None
    for j in range(blocks):
        part = jnp.dot(query, qkv_ref[j, 1], preferred_element_type=jnp.float32)
        scores[:, j * rows : (j + 1) * rows] = part
        for first in range(0, rows, 128):
            piece = part[:, first : first + 128]
            top = piece if top is None else jnp.maximum(top, piece)
    top = jnp.max(top, axis=-1, keepdims=True)
    total = jnp.zeros((rows, 2 * dim), jnp.float32)
    for j in range(blocks):
        weights = jnp.exp(scores[:, j * rows : (j + 1) * rows] - top).astype(jnp.bfloat16)
        total = total + jnp.dot(
            weights, value_rows[j * rows : (j + 1) * rows, :], preferred_element_type=jnp.float32
        )
    total = total.T
    out_ref[0] = (total[:dim] / total[dim:]).astype(jnp.bfloat16)


def attend(qkv):
    blocks, _, dim, rows = qkv.shape
    return pl.pallas_call(
        attention_kernel,
        out_shape=jax.ShapeDtypeStruct((blocks, dim, rows), jnp.bfloat16),
        grid=(blocks,),
        in_specs=[pl.BlockSpec(qkv.shape, lambda i: (0, 0, 0, 0))],
        out_specs=pl.BlockSpec((1, dim, rows), lambda i: (i, 0, 0)),
        scratch_shapes=[
            pltpu.VMEM((blocks * rows, 2 * dim), jnp.bfloat16),
            pltpu.VMEM((rows, blocks * rows), jnp.float32),
        ],
        compiler_params=pltpu.CompilerParams(
            dimension_semantics=("arbitrary",), vmem_limit_bytes=48 * 2**20
        ),
        cost_estimate=pl.CostEstimate(
            flops=16 * 2**30, bytes_accessed=3 * 2**20, transcendentals=2**24
        ),
    )(qkv)


def swap(blocks, axis):
    return lax.all_to_all(blocks, axis, split_axis=0, concat_axis=0, tiled=True)


def local(states, start, noise, coefficients, context, qkv_weight, out_weights, gain):
    steps, seqs = lax.axis_size("step"), lax.axis_size("seq")
    step = lax.axis_index("step")
    rows, width = start.shape
    tokens, dim = context.shape[1:]

    first_weight = lax.all_gather(out_weights[0], "step", axis=0, tiled=True)
    whole_qkv = lax.all_gather(qkv_weight, "step", axis=0, tiled=True)
    last_weight = lax.all_gather(out_weights[1], "step", axis=0, tiled=True)

    heads_tokens = context[0].T.reshape(dim, seqs, rows).transpose(1, 0, 2)
    token_context = swap(heads_tokens, "seq").reshape(seqs * dim, rows)

    factors = coefficients[0]
    base = (factors[0] + factors[1]) * states[0] + factors[2] * noise[0].astype(jnp.float32)
    product = lax.dot_general(
        token_context, first_weight, (((0,), (0,)), ((), ())), preferred_element_type=jnp.float32
    )
    drift = base + factors[1] * product

    piece = rows // steps
    drifts = swap(drift.reshape(steps, piece, width), "step")
    running = lax.dynamic_slice_in_dim(start, step * piece, piece, 0)
    advanced = []
    for j in range(steps):
        advanced.append(running)
        running = running + drifts[j]
    advanced = jnp.stack(advanced)
    mean = jnp.mean(advanced, axis=-1, keepdims=True)
    centred = advanced - mean
    variance = jnp.mean(centred * centred, axis=-1, keepdims=True)
    normed = (centred * lax.rsqrt(variance + 1e-05) * gain).astype(jnp.bfloat16)
    normed = swap(normed, "step").reshape(rows, width)
    advanced = swap(advanced, "step").reshape(rows, width)

    qkv = lax.dot_general(
        whole_qkv, normed, (((0,), (1,)), ((), ())), preferred_element_type=jnp.float32
    ).astype(jnp.bfloat16)
    by_head = qkv.reshape(3, seqs, dim, rows).transpose(1, 0, 2, 3)
    attended = attend(swap(by_head, "seq"))
    attended = swap(attended, "seq").reshape(seqs * dim, rows)
    mixed = advanced + lax.dot_general(
        attended, last_weight, (((0,), (0,)), ((), ())), preferred_element_type=jnp.float32
    )
    return (advanced[None], mixed[None])


def solution(mesh):
    placed = (
        P("step", "seq", None),
        P("seq", None),
        P("step", "seq", None),
        P("step", None),
        P("step", None, "seq"),
        P("step", None),
        P(None, "step", None),
        P(),
    )
    return jax.shard_map(
        local,
        mesh=mesh,
        in_specs=placed,
        out_specs=(P("step", "seq", None), P("step", "seq", None)),
        check_vma=False,
    )
```

```python
import jax
import jax.numpy as jnp
from jax import lax
from jax.experimental import pallas as pl
from jax.experimental.pallas import tpu as pltpu
from jax.sharding import PartitionSpec as P

HEAD_DIM = 64
GRANT = 60 * 2**20


def attention_kernel(qkv_ref, out_ref, value_rows, scores):
    block = pl.program_id(0)
    blocks, _, dim, rows = qkv_ref.shape

    @pl.when(block == 0)
    def _():
        for j in range(blocks):
            values = qkv_ref[j, 2].astype(jnp.float32)
            padded = jnp.concatenate([values, jnp.ones((dim, rows), jnp.float32)], axis=0)
            value_rows[j * rows : (j + 1) * rows, :] = padded.T.astype(jnp.bfloat16)

    query = qkv_ref[block, 0].astype(jnp.float32) * (HEAD_DIM**-0.5)
    query = jnp.concatenate([query, query], axis=0).T[:, :dim].astype(jnp.bfloat16)
    top = None
    for j in range(blocks):
        part = jnp.dot(query, qkv_ref[j, 1], preferred_element_type=jnp.float32)
        scores[:, j * rows : (j + 1) * rows] = part
        for first in range(0, rows, 128):
            piece = part[:, first : first + 128]
            top = piece if top is None else jnp.maximum(top, piece)
    top = jnp.max(top, axis=-1, keepdims=True)
    total = jnp.zeros((rows, 2 * dim), jnp.float32)
    for j in range(blocks):
        weights = jnp.exp(scores[:, j * rows : (j + 1) * rows] - top).astype(jnp.bfloat16)
        total = total + jnp.dot(
            weights, value_rows[j * rows : (j + 1) * rows, :], preferred_element_type=jnp.float32
        )
    total = total.T
    out_ref[0] = (total[:dim] / total[dim:]).astype(jnp.bfloat16)


def attend(qkv):
    blocks, _, dim, rows = qkv.shape
    return pl.pallas_call(
        attention_kernel,
        out_shape=jax.ShapeDtypeStruct((blocks, dim, rows), jnp.bfloat16),
        grid=(blocks,),
        in_specs=[pl.BlockSpec(qkv.shape, lambda i: (0, 0, 0, 0))],
        out_specs=pl.BlockSpec((1, dim, rows), lambda i: (i, 0, 0)),
        scratch_shapes=[
            pltpu.VMEM((blocks * rows, 2 * dim), jnp.bfloat16),
            pltpu.VMEM((rows, blocks * rows), jnp.float32),
        ],
        compiler_params=pltpu.CompilerParams(
            dimension_semantics=("arbitrary",), vmem_limit_bytes=48 * 2**20
        ),
        cost_estimate=pl.CostEstimate(
            flops=16 * 2**30, bytes_accessed=3 * 2**20, transcendentals=2**24
        ),
    )(qkv)


def cut_kernel(
    place_ref, context_ref, qkv_ref, weights_ref, first_ref, qkv_half_ref, last_ref, *refs
):
    *pieces, context, qkv_half, shard, last, done = refs
    core, chip = place_ref[0], place_ref[1]
    chips = len(pieces) + 1
    half, width = first_ref.shape[2], pieces[0].shape[1]
    columns = qkv_half_ref.shape[1]
    loads = [
        pltpu.make_async_copy(
            qkv_ref.at[:, pl.ds(pl.multiple_of(core * columns, columns), columns)],
            qkv_half,
            done.at[0],
        ),
        pltpu.make_async_copy(
            weights_ref.at[0, :, pl.ds(pl.multiple_of(core * half, half), half)], shard, done.at[1]
        ),
        pltpu.make_async_copy(context_ref, context, done.at[2]),
        pltpu.make_async_copy(weights_ref.at[1], last, done.at[3]),
    ]
    for load in loads:
        load.start()
    stores = [pltpu.make_async_copy(qkv_half, qkv_half_ref, done.at[4])]
    loads[0].wait()
    stores[-1].start()
    loads[1].wait()
    for i in range(first_ref.shape[0]):
        stores.append(pltpu.make_async_copy(shard, first_ref.at[i], done.at[6 + chips + i]))
        stores[-1].start()
    loads[2].wait()
    for k, piece in enumerate(pieces):
        target = lax.rem(chip + k + 1, chips)
        tokens = pl.ds(pl.multiple_of(target * width, width), width)
        stores.append(pltpu.make_async_copy(context.at[:, tokens], piece, done.at[6 + k]))
        stores[-1].start()
    loads[3].wait()
    stores.append(pltpu.make_async_copy(last, last_ref, done.at[5]))
    stores[-1].start()
    for store in stores:
        store.wait()


def cut(place, context, qkv_weight, out_weights, steps, chips):
    dim, tokens = context.shape
    _, depth, width = out_weights.shape
    scalars = pl.BlockSpec(memory_space=pltpu.SMEM)
    far = pl.BlockSpec(memory_space=pl.ANY)
    shapes = [
        (steps, depth, width // 2),
        (qkv_weight.shape[0], qkv_weight.shape[1] // 2),
        (depth, width),
    ] + [(dim, tokens // chips)] * (chips - 1)
    return pl.pallas_call(
        cut_kernel,
        out_shape=[jax.ShapeDtypeStruct(shape, jnp.bfloat16) for shape in shapes],
        in_specs=[scalars] + [far] * 3,
        out_specs=[far] * len(shapes),
        scratch_shapes=[
            pltpu.VMEM(context.shape, jnp.bfloat16),
            pltpu.VMEM(shapes[1], jnp.bfloat16),
            pltpu.VMEM(shapes[0][1:], jnp.bfloat16),
            pltpu.VMEM(shapes[2], jnp.bfloat16),
            pltpu.SemaphoreType.DMA((6 + chips + steps,)),
        ],
        compiler_params=pltpu.CompilerParams(vmem_limit_bytes=GRANT),
        cost_estimate=pl.CostEstimate(flops=0, bytes_accessed=4 * 2**20, transcendentals=0),
    )(place, context, qkv_weight, out_weights)


def collect_kernel(place_ref, context_ref, *refs):
    *pieces, weight_ref, kept_ref, given_ref, _ = refs
    core, chip = place_ref[0], place_ref[1]
    chips = len(pieces) + 1
    rows = kept_ref.shape[2]
    for k, piece in enumerate((context_ref, *pieces)):
        source = lax.rem(chip - k + chips, chips)
        for side, out_ref in ((core, kept_ref), (1 - core, given_ref)):
            first = side * rows + (2 * rows * chip if k == 0 else 0)
            out_ref[source] = piece[:, pl.ds(pl.multiple_of(first, rows), rows)]


def collect(place, context, pieces, weight):
    dim, width = pieces[0].shape
    chips = len(pieces) + 1
    whole = pl.BlockSpec(memory_space=pltpu.VMEM)
    far = pl.BlockSpec(memory_space=pl.ANY)
    return pl.pallas_call(
        collect_kernel,
        out_shape=(jax.ShapeDtypeStruct((chips, dim, width // 2), jnp.bfloat16),) * 2
        + (jax.ShapeDtypeStruct(weight.shape, weight.dtype),),
        in_specs=[pl.BlockSpec(memory_space=pltpu.SMEM)] + [whole] * chips + [far],
        out_specs=(whole, whole, far),
        input_output_aliases={chips + 1: 2},
        compiler_params=pltpu.CompilerParams(vmem_limit_bytes=8 * 2**20),
        cost_estimate=pl.CostEstimate(flops=0, bytes_accessed=2**20, transcendentals=0),
    )(place, context, *pieces, weight)


def drift_kernel(
    place_ref, factors_ref, kept_ref, taken_ref, mine_ref, other_ref, states_ref, noise_ref,
    drift_ref, context,
):
    core = place_ref[0]
    half = mine_ref.shape[1]
    chips, _, dim, rows = context.shape
    context[:, core] = kept_ref[...]
    context[:, 1 - core] = taken_ref[...]
    token_rows = context[...].reshape(chips * 2 * dim, rows).T
    for side, weight_ref in ((core, mine_ref), (1 - core, other_ref)):
        product = jnp.dot(token_rows, weight_ref[...], preferred_element_type=jnp.float32)
        columns = pl.ds(pl.multiple_of(side * half, half), half)
        drift_ref[:, columns] = (
            (factors_ref[0] + factors_ref[1]) * states_ref[:, columns]
            + factors_ref[1] * product
            + factors_ref[2] * noise_ref[:, columns].astype(jnp.float32)
        )


def drift_of(place, factors, kept, taken, mine, other, states, noise):
    chips, dim, rows = kept.shape
    scalars = pl.BlockSpec(memory_space=pltpu.SMEM)
    whole = pl.BlockSpec(memory_space=pltpu.VMEM)
    return pl.pallas_call(
        drift_kernel,
        out_shape=jax.ShapeDtypeStruct(states.shape, jnp.float32),
        in_specs=[scalars] * 2 + [whole] * 6,
        out_specs=whole,
        scratch_shapes=[pltpu.VMEM((chips, 2, dim, rows), jnp.bfloat16)],
        compiler_params=pltpu.CompilerParams(vmem_limit_bytes=16 * 2**20),
        cost_estimate=pl.CostEstimate(
            flops=2 * mine.shape[0] * states.size, bytes_accessed=8 * 2**20, transcendentals=0
        ),
    )(place, factors, kept, taken, mine, other, states, noise)


def sum_norm_kernel(
    drifts_ref, start_ref, gain_ref, advanced_ref, normed_ref, done_ref, advanced, normed, sent
):
    done_ref[...] = jnp.zeros_like(done_ref)
    running = start_ref[...]
    gain = gain_ref[...]
    for j in range(drifts_ref.shape[0]):
        advanced[j] = running
        mean = jnp.mean(running, axis=-1, keepdims=True)
        centred = running - mean
        variance = jnp.mean(centred * centred, axis=-1, keepdims=True)
        normed[j] = (centred * lax.rsqrt(variance + 1e-05) * gain).astype(jnp.bfloat16)
        running = running + drifts_ref[j]
    stores = (
        pltpu.make_async_copy(normed, normed_ref, sent.at[0]),
        pltpu.make_async_copy(advanced, advanced_ref, sent.at[1]),
    )
    for store in stores:
        store.start()
    for store in stores:
        store.wait()


def sum_norm(drifts, start, gain):
    whole = pl.BlockSpec(memory_space=pltpu.VMEM)
    far = pl.BlockSpec(memory_space=pl.ANY)
    return pl.pallas_call(
        sum_norm_kernel,
        out_shape=(
            jax.ShapeDtypeStruct(drifts.shape, jnp.float32),
            jax.ShapeDtypeStruct(drifts.shape, jnp.bfloat16),
            jax.ShapeDtypeStruct((8, 128), jnp.float32),
        ),
        in_specs=[whole] * 3,
        out_specs=(far, far, whole),
        scratch_shapes=[
            pltpu.VMEM(drifts.shape, jnp.float32),
            pltpu.VMEM(drifts.shape, jnp.bfloat16),
            pltpu.SemaphoreType.DMA((2,)),
        ],
        compiler_params=pltpu.CompilerParams(vmem_limit_bytes=16 * 2**20),
        cost_estimate=pl.CostEstimate(
            flops=16 * drifts.size, bytes_accessed=10 * drifts.size, transcendentals=0
        ),
    )(drifts, start, gain.reshape(1, -1))


def qkv_kernel(
    core_ref, normed_ref, mine_ref, other_ref, out_ref, normed, weights, projected, done, sent
):
    _, _, dim, rows = out_ref.shape
    chunks = weights.shape[0] // 2
    wide = weights.shape[2]
    load_rows = pltpu.make_async_copy(normed_ref, normed, done.at[2 * chunks])
    load_rows.start()
    loads = []
    for side, weight_ref in enumerate((mine_ref, other_ref)):
        for b in range(chunks):
            slot = side * chunks + b
            loads.append(
                pltpu.make_async_copy(
                    weight_ref.at[:, b * wide : (b + 1) * wide], weights.at[slot], done.at[slot]
                )
            )
            loads[-1].start()
    load_rows.wait()
    stores = []
    parts = wide // (4 * dim)
    for slot, load in enumerate(loads):
        load.wait()
        place = lax.rem(core_ref[0] + slot // chunks, 2)
        for b in range(parts):
            part = jnp.dot(
                normed[...],
                weights[slot, :, b * 4 * dim : (b + 1) * 4 * dim],
                preferred_element_type=jnp.float32,
            )
            group = chunks * parts * place + parts * (slot % chunks) + b
            heads = pl.ds(4 * lax.rem(group, 4), 4)
            kind = lax.div(group, 4)
            projected[heads, kind] = part.T.astype(jnp.bfloat16).reshape(4, dim, rows)
            stores.append(
                pltpu.make_async_copy(
                    projected.at[heads, kind], out_ref.at[heads, kind], sent.at[len(stores)]
                )
            )
            stores[-1].start()
    for store in stores:
        store.wait()


def project_qkv(core, normed, mine, other, heads):
    rows, width = normed.shape
    wide = 8 * HEAD_DIM
    chunks = mine.shape[1] // wide
    shape = (heads, 3, HEAD_DIM, rows)
    far = pl.BlockSpec(memory_space=pl.ANY)
    return pl.pallas_call(
        qkv_kernel,
        out_shape=jax.ShapeDtypeStruct(shape, jnp.bfloat16),
        in_specs=[pl.BlockSpec(memory_space=pltpu.SMEM)] + [far] * 3,
        out_specs=far,
        scratch_shapes=[
            pltpu.VMEM(normed.shape, jnp.bfloat16),
            pltpu.VMEM((2 * chunks, width, wide), jnp.bfloat16),
            pltpu.VMEM(shape, jnp.bfloat16),
            pltpu.SemaphoreType.DMA((2 * chunks + 1,)),
            pltpu.SemaphoreType.DMA((4 * chunks,)),
        ],
        compiler_params=pltpu.CompilerParams(vmem_limit_bytes=GRANT),
        cost_estimate=pl.CostEstimate(
            flops=6 * rows * width * heads * HEAD_DIM, bytes_accessed=10 * 2**20, transcendentals=0
        ),
    )(core, normed, mine, other)


def mix_kernel(
    attended_ref, weight_ref, advanced_ref, copied_ref, mixed_ref,
    attended, weight, advanced, mixed, done, sent,
):
    rows, width = advanced.shape
    chunks = weight.shape[0]
    wide = width // chunks
    load_attended = pltpu.make_async_copy(attended_ref, attended, done.at[chunks])
    load_advanced = pltpu.make_async_copy(advanced_ref, advanced, done.at[chunks + 1])
    loads = [
        pltpu.make_async_copy(weight_ref.at[:, b * wide : (b + 1) * wide], weight.at[b], done.at[b])
        for b in range(chunks)
    ]
    for load in (load_attended, *loads, load_advanced):
        load.start()
    load_attended.wait()
    token_rows = attended[...].T
    stores = []
    for b in range(chunks):
        columns = slice(b * wide, (b + 1) * wide)
        loads[b].wait()
        product = jnp.dot(token_rows, weight[b], preferred_element_type=jnp.float32)
        if b == 0:
            load_advanced.wait()
            stores.append(pltpu.make_async_copy(advanced, copied_ref, sent.at[chunks]))
            stores[-1].start()
        mixed[:, columns] = advanced[:, columns] + product
        stores.append(
            pltpu.make_async_copy(mixed.at[:, columns], mixed_ref.at[:, columns], sent.at[b])
        )
        stores[-1].start()
    for store in stores:
        store.wait()


def mix(attended, weight, advanced):
    depth, rows = attended.shape
    width = advanced.shape[1]
    chunks = width // 256
    far = pl.BlockSpec(memory_space=pl.ANY)
    return pl.pallas_call(
        mix_kernel,
        out_shape=(jax.ShapeDtypeStruct(advanced.shape, jnp.float32),) * 2,
        in_specs=[far] * 3,
        out_specs=(far, far),
        scratch_shapes=[
            pltpu.VMEM(attended.shape, jnp.bfloat16),
            pltpu.VMEM((chunks, depth, width // chunks), jnp.bfloat16),
            pltpu.VMEM(advanced.shape, jnp.float32),
            pltpu.VMEM(advanced.shape, jnp.float32),
            pltpu.SemaphoreType.DMA((chunks + 2,)),
            pltpu.SemaphoreType.DMA((chunks + 1,)),
        ],
        compiler_params=pltpu.CompilerParams(vmem_limit_bytes=GRANT),
        cost_estimate=pl.CostEstimate(
            flops=2 * rows * depth * width, bytes_accessed=8 * 2**20, transcendentals=0
        ),
    )(attended, weight, advanced)


def after_kernel(*refs):
    pass


def after(array, other):
    anywhere = pl.BlockSpec(memory_space=pltpu.HBM)
    return pl.pallas_call(
        after_kernel,
        out_shape=jax.ShapeDtypeStruct(array.shape, array.dtype),
        in_specs=[anywhere, anywhere],
        out_specs=anywhere,
        input_output_aliases={0: 0},
        cost_estimate=pl.CostEstimate(flops=0, bytes_accessed=0, transcendentals=0),
    )(array, other)


def swap(blocks, axis):
    return lax.all_to_all(blocks, axis, split_axis=0, concat_axis=0, tiled=True)


def local(states, start, noise, coefficients, context, qkv_weight, out_weights, gain):
    steps, seqs = lax.axis_size("step"), lax.axis_size("seq")
    step, seq = lax.axis_index("step"), lax.axis_index("seq")
    rows, width = start.shape
    tokens, dim = context.shape[1:]

    heads, chips = seqs, seqs // 2
    core, chip = lax.rem(seq, 2), lax.div(seq, 2)
    place = jnp.stack([core, chip]).astype(jnp.int32)
    pairs = [(i, i ^ 1) for i in range(seqs)]
    heads_tokens = context[0].T

    first_half, qkv_half, last_shard, *pieces = cut(
        place, heads_tokens, qkv_weight, out_weights, steps, chips
    )
    qkv_mine = lax.all_gather(qkv_half, "step", axis=0, tiled=True)
    mine = swap(first_half, "step").reshape(-1, width // 2)

    pieces = [
        lax.ppermute(piece, "seq", [(i, (i + 2 * k + 2) % seqs) for i in range(seqs)])
        for k, piece in enumerate(pieces)
    ]
    kept, given, mine = collect(place, heads_tokens, pieces, mine)
    taken = lax.ppermute(given, "seq", pairs)
    other = lax.ppermute(mine, "seq", pairs)
    drift = drift_of(place, coefficients[0], kept, taken, mine, other, states[0], noise[0])

    piece = rows // steps
    drifts = swap(drift.reshape(steps, piece, width), "step")
    advanced, normed, summed = sum_norm(
        drifts, lax.dynamic_slice_in_dim(start, step * piece, piece, 0), gain
    )
    qkv_mine = after(qkv_mine, summed)
    qkv_other = lax.ppermute(qkv_mine, "seq", pairs)
    normed = swap(normed, "step").reshape(rows, width)

    by_head = swap(project_qkv(place, normed, qkv_mine, qkv_other, heads), "seq")
    advanced = swap(after(advanced, by_head[0, 0, :16, :128]), "step").reshape(rows, width)
    last_weight = lax.all_gather(last_shard, "step", axis=0, tiled=True)
    attended = after(attend(by_head), advanced)
    attended = swap(attended, "seq").reshape(seqs * dim, rows)
    advanced, mixed = mix(attended, last_weight, advanced)
    return (advanced[None], mixed[None])


def solution(mesh):
    placed = (
        P("step", "seq", None),
        P("seq", None),
        P("step", "seq", None),
        P("step", None),
        P("step", None, "seq"),
        P("step", None),
        P(None, "step", None),
        P(),
    )
    return jax.shard_map(
        local,
        mesh=mesh,
        in_specs=placed,
        out_specs=(P("step", "seq", None), P("step", "seq", None)),
        check_vma=False,
    )
```

```python
import jax
import jax.numpy as jnp
from jax import lax
from jax.experimental import pallas as pl
from jax.experimental.pallas import tpu as pltpu
from jax.sharding import PartitionSpec as P

HEAD_DIM = 64
GRANT = 60 * 2**20


def attention_kernel(qkv_ref, out_ref, value_rows, scores, tops):
    turn, turns = pl.program_id(0), pl.num_programs(0)
    blocks, _, dim, rows = qkv_ref.shape
    taken = out_ref.shape[0]

    @pl.when(turn == 0)
    def _():
        for j in range(blocks):
            values = qkv_ref[j, 2].astype(jnp.float32)
            padded = jnp.concatenate([values, jnp.ones((dim, rows), jnp.float32)], axis=0)
            value_rows[j * rows : (j + 1) * rows, :] = padded.T.astype(jnp.bfloat16)

    def score(which, slot):
        queries = []
        for b in range(taken):
            query = qkv_ref[which * taken + b, 0].astype(jnp.float32) * (HEAD_DIM**-0.5)
            query = jnp.concatenate([query, query], axis=0).T[:, :dim]
            queries.append(query.astype(jnp.bfloat16))
        queries = jnp.concatenate(queries, axis=0)
        top = None
        for j in range(blocks):
            part = jnp.dot(queries, qkv_ref[j, 1], preferred_element_type=jnp.float32)
            scores[slot, :, j * rows : (j + 1) * rows] = part
            for first in range(0, rows, 128):
                piece = part[:, first : first + 128]
                top = piece if top is None else jnp.maximum(top, piece)
        tops[slot] = jnp.broadcast_to(jnp.max(top, axis=-1, keepdims=True), top.shape)

    def finish(slot):
        top = tops[slot][:, :1]
        total = jnp.zeros((taken * rows, 2 * dim), jnp.float32)
        for j in range(blocks):
            keys = slice(j * rows, (j + 1) * rows)
            weights = jnp.exp(scores[slot, :, keys] - top).astype(jnp.bfloat16)
            total = total + jnp.dot(weights, value_rows[keys, :], preferred_element_type=jnp.float32)
        total = total.T
        attended = (total[:dim] / total[dim:]).astype(jnp.bfloat16)
        for b in range(taken):
            out_ref[b] = attended[:, b * rows : (b + 1) * rows]

    @pl.when(turn == 0)
    def _():
        score(0, 0)

    for slot in (0, 1):

        @pl.when((lax.rem(turn, 2) == slot) & (turn < turns - 1))
        def _():
            score(turn + 1, 1 - slot)
            finish(slot)

        @pl.when((lax.rem(turn, 2) == slot) & (turn == turns - 1))
        def _():
            finish(slot)


def attend(qkv):
    blocks, _, dim, rows = qkv.shape
    taken = 4
    return pl.pallas_call(
        attention_kernel,
        out_shape=jax.ShapeDtypeStruct((blocks, dim, rows), jnp.bfloat16),
        grid=(blocks // taken,),
        in_specs=[pl.BlockSpec(qkv.shape, lambda i: (0, 0, 0, 0))],
        out_specs=pl.BlockSpec((taken, dim, rows), lambda i: (i, 0, 0)),
        scratch_shapes=[
            pltpu.VMEM((blocks * rows, 2 * dim), jnp.bfloat16),
            pltpu.VMEM((2, taken * rows, blocks * rows), jnp.float32),
            pltpu.VMEM((2, taken * rows, 128), jnp.float32),
        ],
        compiler_params=pltpu.CompilerParams(
            dimension_semantics=("arbitrary",), vmem_limit_bytes=48 * 2**20
        ),
        cost_estimate=pl.CostEstimate(
            flops=16 * 2**30, bytes_accessed=3 * 2**20, transcendentals=2**24
        ),
    )(qkv)


def position(seq_ref):
    return lax.rem(seq_ref[0], 2), lax.div(seq_ref[0], 2)


def tiles(count):
    for n in range(3 * count):
        yield slice(16 * (n // 3), 16 * (n // 3) + 16), 128 * (n % 3), 16 * (n // 5), 128 * (n % 5)


def cut_kernel(seq_ref, context_ref, qkv_ref, weights_ref, first_ref, last_ref, *refs):
    *pieces, context, shard, last, done, sent = refs
    core, chip = position(seq_ref)
    chips = len(pieces) + 1
    depth, half, width = weights_ref.shape[1], first_ref.shape[2], pieces[0].shape[1]
    inner = qkv_ref.shape[1] // 3
    shard[depth:, :] = jnp.zeros((shard.shape[0] - depth, half), jnp.bfloat16)
    loads = [
        pltpu.make_async_copy(
            weights_ref.at[0, :, pl.ds(pl.multiple_of(core * half, half), half)],
            shard.at[:depth],
            done.at[0],
        )
    ]
    for n, (rows, column, low, left) in enumerate(tiles(3)):
        first_row = pl.multiple_of(32 * core + rows.start, 16)
        first_column = pl.multiple_of(column // 128 * inner + 128 * chip, 128)
        loads.append(
            pltpu.make_async_copy(
                qkv_ref.at[pl.ds(first_row, 16), pl.ds(first_column, 128)],
                shard.at[depth + low : depth + low + 16, left : left + 128],
                done.at[3 + n],
            )
        )
    load_context = pltpu.make_async_copy(context_ref, context, done.at[1])
    load_last = pltpu.make_async_copy(weights_ref.at[1], last, done.at[2])
    for load in (*loads, load_context, load_last):
        load.start()
    for load in loads:
        load.wait()
    stores = []
    for i in range(first_ref.shape[0]):
        stores.append(pltpu.make_async_copy(shard, first_ref.at[i], sent.at[chips + i]))
        stores[-1].start()
    load_context.wait()
    for k, piece in enumerate(pieces):
        target = lax.rem(chip + k + 1, chips)
        tokens = pl.ds(pl.multiple_of(target * width, width), width)
        stores.append(pltpu.make_async_copy(context.at[:, tokens], piece, sent.at[k]))
        stores[-1].start()
    load_last.wait()
    stores.append(pltpu.make_async_copy(last, last_ref, sent.at[chips - 1]))
    stores[-1].start()
    for store in stores:
        store.wait()


def cut(seq, context, qkv_weight, out_weights, steps, chips):
    dim, tokens = context.shape
    _, depth, width = out_weights.shape
    far = pl.BlockSpec(memory_space=pl.ANY)
    shapes = [(steps, depth + 32, width // 2), (depth, width)] + [(dim, tokens // chips)] * (chips - 1)
    return pl.pallas_call(
        cut_kernel,
        out_shape=[jax.ShapeDtypeStruct(shape, jnp.bfloat16) for shape in shapes],
        in_specs=[pl.BlockSpec(memory_space=pltpu.SMEM)] + [far] * 3,
        out_specs=[far] * len(shapes),
        scratch_shapes=[
            pltpu.VMEM(context.shape, jnp.bfloat16),
            pltpu.VMEM(shapes[0][1:], jnp.bfloat16),
            pltpu.VMEM(shapes[1], jnp.bfloat16),
            pltpu.SemaphoreType.DMA((12,)),
            pltpu.SemaphoreType.DMA((chips + steps,)),
        ],
        compiler_params=pltpu.CompilerParams(vmem_limit_bytes=GRANT),
        cost_estimate=pl.CostEstimate(flops=0, bytes_accessed=4 * 2**20, transcendentals=0),
    )(seq, context, qkv_weight, out_weights)


def collect_kernel(seq_ref, context_ref, *refs):
    *pieces, packed_ref, kept_ref, given_ref, slices_ref, _, arrived, slices, done, sent = refs
    core, chip = position(seq_ref)
    chips = len(pieces) + 1
    rows = kept_ref.shape[2]
    depth = packed_ref.shape[1] - 32
    own = context_ref.at[:, pl.ds(pl.multiple_of(2 * rows * chip, 2 * rows), 2 * rows)]
    loads = []
    for k, piece in enumerate((own, *pieces)):
        source = lax.rem(chip - k + chips, chips)
        loads.append(pltpu.make_async_copy(piece, arrived.at[source], done.at[9 + k]))
        loads[-1].start()
    unpacks = []
    for n, (place, column, low, left) in enumerate(tiles(3)):
        unpacks.append(
            pltpu.make_async_copy(
                packed_ref.at[:, depth + low : depth + low + 16, left : left + 128],
                slices.at[:, place, column : column + 128],
                done.at[n],
            )
        )
        unpacks[-1].start()
    for load in loads:
        load.wait()
    stores = []
    for turn, (side, out_ref) in enumerate(((1 - core, given_ref), (core, kept_ref))):
        tokens = pl.ds(pl.multiple_of(side * rows, rows), rows)
        stores.append(pltpu.make_async_copy(arrived.at[:, :, tokens], out_ref, sent.at[turn]))
        stores[-1].start()
    for unpack in unpacks:
        unpack.wait()
    stores.append(pltpu.make_async_copy(slices, slices_ref, sent.at[2]))
    stores[-1].start()
    for store in stores:
        store.wait()


def collect(seq, context, pieces, packed):
    dim, width = pieces[0].shape
    chips = len(pieces) + 1
    shape = (packed.shape[0], 48, 384)
    far = pl.BlockSpec(memory_space=pl.ANY)
    return pl.pallas_call(
        collect_kernel,
        out_shape=(jax.ShapeDtypeStruct((chips, dim, width // 2), jnp.bfloat16),) * 2
        + (
            jax.ShapeDtypeStruct(shape, jnp.bfloat16),
            jax.ShapeDtypeStruct(packed.shape, jnp.bfloat16),
        ),
        in_specs=[pl.BlockSpec(memory_space=pltpu.SMEM)] + [far] * (chips + 1),
        out_specs=(far,) * 4,
        input_output_aliases={chips + 1: 3},
        scratch_shapes=[
            pltpu.VMEM((chips, dim, width), jnp.bfloat16),
            pltpu.VMEM(shape, jnp.bfloat16),
            pltpu.SemaphoreType.DMA((9 + chips,)),
            pltpu.SemaphoreType.DMA((3,)),
        ],
        compiler_params=pltpu.CompilerParams(vmem_limit_bytes=GRANT),
        cost_estimate=pl.CostEstimate(flops=0, bytes_accessed=2**20, transcendentals=0),
    )(seq, context, *pieces, packed)


def drift_kernel(
    seq_ref, factors_ref, kept_ref, taken_ref, mine_ref, other_ref, states_ref, noise_ref,
    drift_ref, context, weights, states, noise, drift, done,
):
    core, _ = position(seq_ref)
    chips, _, dim, rows = context.shape
    half = weights.shape[3]
    loads = [
        pltpu.make_async_copy(kept_ref, context.at[:, core], done.at[0]),
        pltpu.make_async_copy(taken_ref, context.at[:, 1 - core], done.at[1]),
        pltpu.make_async_copy(mine_ref.at[:, :dim, :], weights.at[0], done.at[2]),
        pltpu.make_async_copy(other_ref.at[:, :dim, :], weights.at[1], done.at[3]),
        pltpu.make_async_copy(states_ref, states, done.at[4]),
        pltpu.make_async_copy(noise_ref, noise, done.at[5]),
    ]
    for load in loads:
        load.start()
    loads[0].wait()
    loads[1].wait()
    token_rows = context[...].reshape(chips * 2 * dim, rows).T
    stores = []
    for turn, side in enumerate((core, 1 - core)):
        loads[2 + turn].wait()
        weight = weights[turn].reshape(chips * 2 * dim, half)
        product = jnp.dot(token_rows, weight, preferred_element_type=jnp.float32)
        if turn == 0:
            loads[4].wait()
            loads[5].wait()
        columns = pl.ds(pl.multiple_of(side * half, half), half)
        drift[:, columns] = (
            (factors_ref[0] + factors_ref[1]) * states[:, columns]
            + factors_ref[1] * product
            + factors_ref[2] * noise[:, columns].astype(jnp.float32)
        )
        stores.append(
            pltpu.make_async_copy(drift.at[:, columns], drift_ref.at[:, columns], done.at[6 + turn])
        )
        stores[-1].start()
    for store in stores:
        store.wait()


def drift_of(seq, factors, kept, taken, mine, other, states, noise):
    chips, dim, rows = kept.shape
    scalars = pl.BlockSpec(memory_space=pltpu.SMEM)
    far = pl.BlockSpec(memory_space=pl.ANY)
    return pl.pallas_call(
        drift_kernel,
        out_shape=jax.ShapeDtypeStruct(states.shape, jnp.float32),
        in_specs=[scalars] * 2 + [far] * 6,
        out_specs=far,
        scratch_shapes=[
            pltpu.VMEM((chips, 2, dim, rows), jnp.bfloat16),
            pltpu.VMEM((2, mine.shape[0], dim, mine.shape[2]), jnp.bfloat16),
            pltpu.VMEM(states.shape, jnp.float32),
            pltpu.VMEM(states.shape, jnp.bfloat16),
            pltpu.VMEM(states.shape, jnp.float32),
            pltpu.SemaphoreType.DMA((8,)),
        ],
        compiler_params=pltpu.CompilerParams(vmem_limit_bytes=GRANT),
        cost_estimate=pl.CostEstimate(
            flops=2**11 * states.size, bytes_accessed=8 * 2**20, transcendentals=0
        ),
    )(seq, factors, kept, taken, mine, other, states, noise)


def sum_kernel(drifts_ref, start_ref, advanced_ref):
    running = start_ref[...]
    for j in range(drifts_ref.shape[0]):
        advanced_ref[j] = running
        running = running + drifts_ref[j]


def sum_before(drifts, start):
    whole = pl.BlockSpec(memory_space=pltpu.VMEM)
    return pl.pallas_call(
        sum_kernel,
        out_shape=jax.ShapeDtypeStruct(drifts.shape, jnp.float32),
        in_specs=[whole] * 2,
        out_specs=whole,
        compiler_params=pltpu.CompilerParams(vmem_limit_bytes=16 * 2**20),
        cost_estimate=pl.CostEstimate(
            flops=drifts.size, bytes_accessed=8 * drifts.size, transcendentals=0
        ),
    )(drifts, start)


def qkv_kernel(
    advanced_ref, gain_ref, slices_ref, out_ref, advanced, normed, weights, projected, done, sent
):
    _, _, dim, rows = out_ref.shape
    chips = slices_ref.shape[0] // 2
    steps, depth, _ = weights.shape
    columns, upper = slices_ref.shape[3], slices_ref.shape[2]
    load_rows = pltpu.make_async_copy(advanced_ref, advanced, done.at[2 * chips])
    load_rows.start()
    loads = []
    for c in range(chips):
        place = slice(c * columns, (c + 1) * columns)
        rest = depth - upper
        loads.append(
            (
                pltpu.make_async_copy(
                    slices_ref.at[2 * c], weights.at[:, :upper, place], done.at[2 * c]
                ),
                pltpu.make_async_copy(
                    slices_ref.at[2 * c + 1, :, upper - rest :],
                    weights.at[:, upper:, place],
                    done.at[2 * c + 1],
                ),
            )
        )
    for pair in loads[:4]:
        for load in pair:
            load.start()
    load_rows.wait()
    gain = gain_ref[...]
    part_rows = 32
    for first in range(0, rows, part_rows):
        some = advanced[first : first + part_rows, :]
        mean = jnp.mean(some, axis=-1, keepdims=True)
        centred = some - mean
        variance = jnp.mean(centred * centred, axis=-1, keepdims=True)
        normed[first : first + part_rows, :] = (
            centred * lax.rsqrt(variance + 1e-05) * gain
        ).astype(jnp.bfloat16)
    stores = []
    for c in range(0, chips, 2):
        for pair in loads[c : c + 2]:
            for load in pair:
                load.wait()
        for pair in loads[c + 4 : c + 6]:
            for load in pair:
                load.start()
        weight = weights[:, :, c * columns : (c + 2) * columns].reshape(steps * depth, 2 * columns)
        part = jnp.dot(normed[...], weight, preferred_element_type=jnp.float32)
        part = part.T.astype(jnp.bfloat16).reshape(2, 3, 2, dim, rows)
        for b in (0, 1):
            for kind in range(3):
                projected[2 * (c + b) : 2 * (c + b) + 2, kind] = part[b, kind]
        heads = slice(2 * c, 2 * c + 4)
        stores.append(
            pltpu.make_async_copy(projected.at[heads], out_ref.at[heads], sent.at[c // 2])
        )
        stores[-1].start()
    for store in stores:
        store.wait()


def project_qkv(advanced, gain, slices, depth, dim):
    rows, width = advanced.shape
    heads, steps, _, columns = slices.shape
    shape = (heads, 3, dim, rows)
    far = pl.BlockSpec(memory_space=pl.ANY)
    return pl.pallas_call(
        qkv_kernel,
        out_shape=jax.ShapeDtypeStruct(shape, jnp.bfloat16),
        in_specs=[far, pl.BlockSpec(memory_space=pltpu.VMEM), far],
        out_specs=far,
        scratch_shapes=[
            pltpu.VMEM(advanced.shape, jnp.float32),
            pltpu.VMEM(advanced.shape, jnp.bfloat16),
            pltpu.VMEM((steps, depth, columns * heads // 2), jnp.bfloat16),
            pltpu.VMEM(shape, jnp.bfloat16),
            pltpu.SemaphoreType.DMA((heads + 1,)),
            pltpu.SemaphoreType.DMA((heads // 4,)),
        ],
        compiler_params=pltpu.CompilerParams(vmem_limit_bytes=GRANT),
        cost_estimate=pl.CostEstimate(
            flops=6 * rows * width * heads * dim, bytes_accessed=10 * 2**20, transcendentals=0
        ),
    )(advanced, gain.reshape(1, -1), slices)


def mix_kernel(
    attended_ref, weight_ref, advanced_ref, copied_ref, mixed_ref,
    weight, advanced, mixed, done, sent,
):
    rows, width = advanced.shape
    chunks = weight.shape[0]
    wide = width // chunks
    load_advanced = pltpu.make_async_copy(advanced_ref, advanced, done.at[chunks + 1])
    loads = [
        pltpu.make_async_copy(weight_ref.at[:, b * wide : (b + 1) * wide], weight.at[b], done.at[b])
        for b in range(chunks)
    ]
    for load in (*loads, load_advanced):
        load.start()
    token_rows = attended_ref[...].T
    stores = []
    for b in range(chunks):
        columns = slice(b * wide, (b + 1) * wide)
        loads[b].wait()
        product = jnp.dot(token_rows, weight[b], preferred_element_type=jnp.float32)
        if b == 0:
            load_advanced.wait()
            stores.append(pltpu.make_async_copy(advanced, copied_ref, sent.at[chunks]))
            stores[-1].start()
        mixed[:, columns] = advanced[:, columns] + product
        stores.append(
            pltpu.make_async_copy(mixed.at[:, columns], mixed_ref.at[:, columns], sent.at[b])
        )
        stores[-1].start()
    for store in stores:
        store.wait()


def mix(attended, weight, advanced):
    depth, rows = attended.shape
    width = advanced.shape[1]
    chunks = width // 256
    far = pl.BlockSpec(memory_space=pl.ANY)
    return pl.pallas_call(
        mix_kernel,
        out_shape=(jax.ShapeDtypeStruct(advanced.shape, jnp.float32),) * 2,
        in_specs=[pl.BlockSpec(memory_space=pltpu.VMEM), far, far],
        out_specs=(far, far),
        scratch_shapes=[
            pltpu.VMEM((chunks, depth, width // chunks), jnp.bfloat16),
            pltpu.VMEM(advanced.shape, jnp.float32),
            pltpu.VMEM(advanced.shape, jnp.float32),
            pltpu.SemaphoreType.DMA((chunks + 2,)),
            pltpu.SemaphoreType.DMA((chunks + 1,)),
        ],
        compiler_params=pltpu.CompilerParams(vmem_limit_bytes=56 * 2**20),
        cost_estimate=pl.CostEstimate(
            flops=2 * rows * depth * width, bytes_accessed=8 * 2**20, transcendentals=0
        ),
    )(attended, weight, advanced)


def swap(blocks, axis):
    return lax.all_to_all(blocks, axis, split_axis=0, concat_axis=0, tiled=True)


def local(states, start, noise, coefficients, context, qkv_weight, out_weights, gain):
    steps, seqs = lax.axis_size("step"), lax.axis_size("seq")
    step, seq = lax.axis_index("step"), lax.axis_index("seq")
    rows, width = start.shape
    tokens, dim = context.shape[1:]

    heads, chips = seqs, seqs // 2
    place = seq.astype(jnp.int32).reshape(1)
    pairs = [(i, i ^ 1) for i in range(seqs)]
    heads_tokens = context[0].T

    first_half, last_shard, *pieces = cut(
        place, heads_tokens, qkv_weight, out_weights, steps, chips
    )
    packed = swap(first_half, "step")

    pieces = [
        lax.ppermute(piece, "seq", [(i, (i + 2 * k + 2) % seqs) for i in range(seqs)])
        for k, piece in enumerate(pieces)
    ]
    kept, given, slices, mine = collect(place, heads_tokens, pieces, packed)
    slices = lax.all_gather(slices, "seq")
    taken = lax.ppermute(given, "seq", pairs)
    other = lax.ppermute(mine, "seq", pairs)
    drift = drift_of(place, coefficients[0], kept, taken, mine, other, states[0], noise[0])

    piece = rows // steps
    drifts = swap(drift.reshape(steps, piece, width), "step")
    advanced = sum_before(drifts, lax.dynamic_slice_in_dim(start, step * piece, piece, 0))
    advanced = swap(advanced, "step").reshape(rows, width)
    by_head = swap(project_qkv(advanced, gain, slices, qkv_weight.shape[0], dim), "seq")
    last_weight = lax.all_gather(last_shard, "step", axis=0, tiled=True)
    attended = swap(attend(by_head), "seq").reshape(seqs * dim, rows)
    advanced, mixed = mix(attended, last_weight, advanced)
    return (advanced[None], mixed[None])


def solution(mesh):
    placed = (
        P("step", "seq", None),
        P("seq", None),
        P("step", "seq", None),
        P("step", None),
        P("step", None, "seq"),
        P("step", None),
        P(None, "step", None),
        P(),
    )
    return jax.shard_map(
        local,
        mesh=mesh,
        in_specs=placed,
        out_specs=(P("step", "seq", None), P("step", "seq", None)),
        check_vma=False,
    )
```

```python
import jax
import jax.numpy as jnp
from jax import lax
from jax.experimental import pallas as pl
from jax.experimental.pallas import tpu as pltpu
from jax.sharding import PartitionSpec as P

HEAD_DIM = 64
GRANT = 60 * 2**20


def attention_kernel(qkv_ref, out_ref, value_rows, scores, tops):
    turn, turns = pl.program_id(0), pl.num_programs(0)
    blocks, _, dim, rows = qkv_ref.shape
    taken = out_ref.shape[0]

    @pl.when(turn == 0)
    def _():
        for j in range(blocks):
            values = qkv_ref[j, 2].astype(jnp.float32)
            padded = jnp.concatenate([values, jnp.ones((dim, rows), jnp.float32)], axis=0)
            value_rows[j * rows : (j + 1) * rows, :] = padded.T.astype(jnp.bfloat16)

    def score(which, slot):
        queries = []
        for b in range(taken):
            query = qkv_ref[which * taken + b, 0].astype(jnp.float32) * (HEAD_DIM**-0.5)
            query = jnp.concatenate([query, query], axis=0).T[:, :dim]
            queries.append(query.astype(jnp.bfloat16))
        queries = jnp.concatenate(queries, axis=0)
        top = None
        for j in range(blocks):
            part = jnp.dot(queries, qkv_ref[j, 1], preferred_element_type=jnp.float32)
            scores[slot, :, j * rows : (j + 1) * rows] = part
            for first in range(0, rows, 128):
                piece = part[:, first : first + 128]
                top = piece if top is None else jnp.maximum(top, piece)
        tops[slot] = jnp.broadcast_to(jnp.max(top, axis=-1, keepdims=True), top.shape)

    def finish(slot):
        top = tops[slot][:, :1]
        total = jnp.zeros((taken * rows, 2 * dim), jnp.float32)
        for j in range(blocks):
            keys = slice(j * rows, (j + 1) * rows)
            weights = jnp.exp(scores[slot, :, keys] - top).astype(jnp.bfloat16)
            total = total + jnp.dot(weights, value_rows[keys, :], preferred_element_type=jnp.float32)
        total = total.T
        attended = (total[:dim] / total[dim:]).astype(jnp.bfloat16)
        for b in range(taken):
            out_ref[b] = attended[:, b * rows : (b + 1) * rows]

    @pl.when(turn == 0)
    def _():
        score(0, 0)

    for slot in (0, 1):

        @pl.when((lax.rem(turn, 2) == slot) & (turn < turns - 1))
        def _():
            score(turn + 1, 1 - slot)
            finish(slot)

        @pl.when((lax.rem(turn, 2) == slot) & (turn == turns - 1))
        def _():
            finish(slot)


def attend(qkv):
    blocks, _, dim, rows = qkv.shape
    taken = 4
    return pl.pallas_call(
        attention_kernel,
        out_shape=jax.ShapeDtypeStruct((blocks, dim, rows), jnp.bfloat16),
        grid=(blocks // taken,),
        in_specs=[pl.BlockSpec(qkv.shape, lambda i: (0, 0, 0, 0))],
        out_specs=pl.BlockSpec((taken, dim, rows), lambda i: (i, 0, 0)),
        scratch_shapes=[
            pltpu.VMEM((blocks * rows, 2 * dim), jnp.bfloat16),
            pltpu.VMEM((2, taken * rows, blocks * rows), jnp.float32),
            pltpu.VMEM((2, taken * rows, 128), jnp.float32),
        ],
        compiler_params=pltpu.CompilerParams(
            dimension_semantics=("arbitrary",), vmem_limit_bytes=48 * 2**20
        ),
        cost_estimate=pl.CostEstimate(
            flops=16 * 2**30, bytes_accessed=3 * 2**20, transcendentals=2**24
        ),
    )(qkv)


def position(seq_ref):
    return lax.rem(seq_ref[0], 2), lax.div(seq_ref[0], 2)


def tiles(count):
    for n in range(3 * count):
        yield slice(16 * (n // 3), 16 * (n // 3) + 16), 128 * (n % 3), 16 * (n // 5), 128 * (n % 5)


def cut_kernel(seq_ref, context_ref, qkv_ref, weights_ref, first_ref, last_ref, *refs):
    *pieces, context, shard, last, done, sent = refs
    core, chip = position(seq_ref)
    chips = len(pieces) + 1
    depth, half, width = weights_ref.shape[1], first_ref.shape[2], pieces[0].shape[1]
    inner = qkv_ref.shape[1] // 3
    shard[depth:, :] = jnp.zeros((shard.shape[0] - depth, half), jnp.bfloat16)
    loads = [
        pltpu.make_async_copy(
            weights_ref.at[0, :, pl.ds(pl.multiple_of(core * half, half), half)],
            shard.at[:depth],
            done.at[0],
        )
    ]
    for n, (rows, column, low, left) in enumerate(tiles(3)):
        first_row = pl.multiple_of(32 * core + rows.start, 16)
        first_column = pl.multiple_of(column // 128 * inner + 128 * chip, 128)
        loads.append(
            pltpu.make_async_copy(
                qkv_ref.at[pl.ds(first_row, 16), pl.ds(first_column, 128)],
                shard.at[depth + low : depth + low + 16, left : left + 128],
                done.at[3 + n],
            )
        )
    load_context = pltpu.make_async_copy(context_ref, context, done.at[1])
    load_last = pltpu.make_async_copy(weights_ref.at[1], last, done.at[2])
    for load in (*loads, load_context, load_last):
        load.start()
    for load in loads:
        load.wait()
    stores = []
    for i in range(first_ref.shape[0]):
        stores.append(pltpu.make_async_copy(shard, first_ref.at[i], sent.at[chips + i]))
        stores[-1].start()
    load_context.wait()
    for k, piece in enumerate(pieces):
        target = lax.rem(chip + k + 1, chips)
        tokens = pl.ds(pl.multiple_of(target * width, width), width)
        stores.append(pltpu.make_async_copy(context.at[:, tokens], piece, sent.at[k]))
        stores[-1].start()
    load_last.wait()
    stores.append(pltpu.make_async_copy(last, last_ref, sent.at[chips - 1]))
    stores[-1].start()
    for store in stores:
        store.wait()


def cut(seq, context, qkv_weight, out_weights, steps, chips):
    dim, tokens = context.shape
    _, depth, width = out_weights.shape
    far = pl.BlockSpec(memory_space=pl.ANY)
    shapes = [(steps, depth + 32, width // 2), (depth, width)] + [(dim, tokens // chips)] * (chips - 1)
    return pl.pallas_call(
        cut_kernel,
        out_shape=[jax.ShapeDtypeStruct(shape, jnp.bfloat16) for shape in shapes],
        in_specs=[pl.BlockSpec(memory_space=pltpu.SMEM)] + [far] * 3,
        out_specs=[far] * len(shapes),
        scratch_shapes=[
            pltpu.VMEM(context.shape, jnp.bfloat16),
            pltpu.VMEM(shapes[0][1:], jnp.bfloat16),
            pltpu.VMEM(shapes[1], jnp.bfloat16),
            pltpu.SemaphoreType.DMA((12,)),
            pltpu.SemaphoreType.DMA((chips + steps,)),
        ],
        compiler_params=pltpu.CompilerParams(vmem_limit_bytes=GRANT),
        cost_estimate=pl.CostEstimate(flops=0, bytes_accessed=4 * 2**20, transcendentals=0),
    )(seq, context, qkv_weight, out_weights)


def collect_kernel(seq_ref, context_ref, *refs):
    *pieces, packed_ref, kept_ref, given_ref, slices_ref, _, arrived, slices, done, sent = refs
    core, chip = position(seq_ref)
    chips = len(pieces) + 1
    rows = kept_ref.shape[2]
    depth = packed_ref.shape[1] - 32
    own = context_ref.at[:, pl.ds(pl.multiple_of(2 * rows * chip, 2 * rows), 2 * rows)]
    loads = []
    for k, piece in enumerate((own, *pieces)):
        source = lax.rem(chip - k + chips, chips)
        loads.append(pltpu.make_async_copy(piece, arrived.at[source], done.at[9 + k]))
        loads[-1].start()
    unpacks = []
    for n, (place, column, low, left) in enumerate(tiles(3)):
        unpacks.append(
            pltpu.make_async_copy(
                packed_ref.at[:, depth + low : depth + low + 16, left : left + 128],
                slices.at[:, place, column : column + 128],
                done.at[n],
            )
        )
        unpacks[-1].start()
    for load in loads:
        load.wait()
    stores = []
    for turn, (side, out_ref) in enumerate(((1 - core, given_ref), (core, kept_ref))):
        tokens = pl.ds(pl.multiple_of(side * rows, rows), rows)
        stores.append(pltpu.make_async_copy(arrived.at[:, :, tokens], out_ref, sent.at[turn]))
        stores[-1].start()
    for unpack in unpacks:
        unpack.wait()
    stores.append(pltpu.make_async_copy(slices, slices_ref, sent.at[2]))
    stores[-1].start()
    for store in stores:
        store.wait()


def collect(seq, context, pieces, packed):
    dim, width = pieces[0].shape
    chips = len(pieces) + 1
    shape = (packed.shape[0], 48, 384)
    far = pl.BlockSpec(memory_space=pl.ANY)
    return pl.pallas_call(
        collect_kernel,
        out_shape=(jax.ShapeDtypeStruct((chips, dim, width // 2), jnp.bfloat16),) * 2
        + (
            jax.ShapeDtypeStruct(shape, jnp.bfloat16),
            jax.ShapeDtypeStruct(packed.shape, jnp.bfloat16),
        ),
        in_specs=[pl.BlockSpec(memory_space=pltpu.SMEM)] + [far] * (chips + 1),
        out_specs=(far,) * 4,
        input_output_aliases={chips + 1: 3},
        scratch_shapes=[
            pltpu.VMEM((chips, dim, width), jnp.bfloat16),
            pltpu.VMEM(shape, jnp.bfloat16),
            pltpu.SemaphoreType.DMA((9 + chips,)),
            pltpu.SemaphoreType.DMA((3,)),
        ],
        compiler_params=pltpu.CompilerParams(vmem_limit_bytes=GRANT),
        cost_estimate=pl.CostEstimate(flops=0, bytes_accessed=2**20, transcendentals=0),
    )(seq, context, *pieces, packed)


def drift_kernel(
    seq_ref, factors_ref, kept_ref, taken_ref, mine_ref, other_ref, states_ref, noise_ref,
    drift_ref, context, weights, states, noise, drift, done,
):
    core, _ = position(seq_ref)
    chips, _, dim, rows = context.shape
    half = weights.shape[3]
    loads = [
        pltpu.make_async_copy(kept_ref, context.at[:, core], done.at[0]),
        pltpu.make_async_copy(taken_ref, context.at[:, 1 - core], done.at[1]),
        pltpu.make_async_copy(mine_ref.at[:, :dim, :], weights.at[0], done.at[2]),
        pltpu.make_async_copy(other_ref.at[:, :dim, :], weights.at[1], done.at[3]),
        pltpu.make_async_copy(states_ref, states, done.at[4]),
        pltpu.make_async_copy(noise_ref, noise, done.at[5]),
    ]
    for load in loads:
        load.start()
    loads[0].wait()
    loads[1].wait()
    token_rows = context[...].reshape(chips * 2 * dim, rows).T
    stores = []
    for turn, side in enumerate((core, 1 - core)):
        loads[2 + turn].wait()
        weight = weights[turn].reshape(chips * 2 * dim, half)
        product = jnp.dot(token_rows, weight, preferred_element_type=jnp.float32)
        if turn == 0:
            loads[4].wait()
            loads[5].wait()
        columns = pl.ds(pl.multiple_of(side * half, half), half)
        drift[:, columns] = (
            (factors_ref[0] + factors_ref[1]) * states[:, columns]
            + factors_ref[1] * product
            + factors_ref[2] * noise[:, columns].astype(jnp.float32)
        )
        stores.append(
            pltpu.make_async_copy(drift.at[:, columns], drift_ref.at[:, columns], done.at[6 + turn])
        )
        stores[-1].start()
    for store in stores:
        store.wait()


def drift_of(seq, factors, kept, taken, mine, other, states, noise):
    chips, dim, rows = kept.shape
    scalars = pl.BlockSpec(memory_space=pltpu.SMEM)
    far = pl.BlockSpec(memory_space=pl.ANY)
    return pl.pallas_call(
        drift_kernel,
        out_shape=jax.ShapeDtypeStruct(states.shape, jnp.float32),
        in_specs=[scalars] * 2 + [far] * 6,
        out_specs=far,
        scratch_shapes=[
            pltpu.VMEM((chips, 2, dim, rows), jnp.bfloat16),
            pltpu.VMEM((2, mine.shape[0], dim, mine.shape[2]), jnp.bfloat16),
            pltpu.VMEM(states.shape, jnp.float32),
            pltpu.VMEM(states.shape, jnp.bfloat16),
            pltpu.VMEM(states.shape, jnp.float32),
            pltpu.SemaphoreType.DMA((8,)),
        ],
        compiler_params=pltpu.CompilerParams(vmem_limit_bytes=GRANT),
        cost_estimate=pl.CostEstimate(
            flops=2**11 * states.size, bytes_accessed=8 * 2**20, transcendentals=0
        ),
    )(seq, factors, kept, taken, mine, other, states, noise)


def sum_kernel(drifts_ref, start_ref, advanced_ref):
    running = start_ref[...]
    for j in range(drifts_ref.shape[0]):
        advanced_ref[j] = running
        running = running + drifts_ref[j]


def sum_before(drifts, start):
    whole = pl.BlockSpec(memory_space=pltpu.VMEM)
    return pl.pallas_call(
        sum_kernel,
        out_shape=jax.ShapeDtypeStruct(drifts.shape, jnp.float32),
        in_specs=[whole] * 2,
        out_specs=whole,
        compiler_params=pltpu.CompilerParams(vmem_limit_bytes=16 * 2**20),
        cost_estimate=pl.CostEstimate(
            flops=drifts.size, bytes_accessed=8 * drifts.size, transcendentals=0
        ),
    )(drifts, start)


def qkv_kernel(
    advanced_ref, gain_ref, slices_ref, out_ref, advanced, normed, weights, projected, done, sent
):
    _, _, dim, rows = out_ref.shape
    chips = slices_ref.shape[0] // 2
    steps, depth, _ = weights.shape
    columns, upper = slices_ref.shape[3], slices_ref.shape[2]
    load_rows = pltpu.make_async_copy(advanced_ref, advanced, done.at[2 * chips])
    load_rows.start()
    loads = []
    for c in range(chips):
        place = slice(c * columns, (c + 1) * columns)
        rest = depth - upper
        loads.append(
            (
                pltpu.make_async_copy(
                    slices_ref.at[2 * c], weights.at[:, :upper, place], done.at[2 * c]
                ),
                pltpu.make_async_copy(
                    slices_ref.at[2 * c + 1, :, upper - rest :],
                    weights.at[:, upper:, place],
                    done.at[2 * c + 1],
                ),
            )
        )
    for pair in loads[:2]:
        for load in pair:
            load.start()
    load_rows.wait()
    for pair in loads[2:4]:
        for load in pair:
            load.start()
    gain = gain_ref[...]
    part_rows = 32
    for first in range(0, rows, part_rows):
        some = advanced[first : first + part_rows, :]
        mean = jnp.mean(some, axis=-1, keepdims=True)
        centred = some - mean
        variance = jnp.mean(centred * centred, axis=-1, keepdims=True)
        normed[first : first + part_rows, :] = (
            centred * lax.rsqrt(variance + 1e-05) * gain
        ).astype(jnp.bfloat16)
    stores = []
    for c in range(0, chips, 2):
        for pair in loads[c : c + 2]:
            for load in pair:
                load.wait()
        for pair in loads[c + 4 : c + 6]:
            for load in pair:
                load.start()
        weight = weights[:, :, c * columns : (c + 2) * columns].reshape(steps * depth, 2 * columns)
        part = jnp.dot(normed[...], weight, preferred_element_type=jnp.float32)
        part = part.T.astype(jnp.bfloat16).reshape(2, 3, 2, dim, rows)
        for b in (0, 1):
            for kind in range(3):
                projected[2 * (c + b) : 2 * (c + b) + 2, kind] = part[b, kind]
        heads = slice(2 * c, 2 * c + 4)
        stores.append(
            pltpu.make_async_copy(projected.at[heads], out_ref.at[heads], sent.at[c // 2])
        )
        stores[-1].start()
    for store in stores:
        store.wait()


def project_qkv(advanced, gain, slices, depth, dim):
    rows, width = advanced.shape
    heads, steps, _, columns = slices.shape
    shape = (heads, 3, dim, rows)
    far = pl.BlockSpec(memory_space=pl.ANY)
    return pl.pallas_call(
        qkv_kernel,
        out_shape=jax.ShapeDtypeStruct(shape, jnp.bfloat16),
        in_specs=[far, pl.BlockSpec(memory_space=pltpu.VMEM), far],
        out_specs=far,
        scratch_shapes=[
            pltpu.VMEM(advanced.shape, jnp.float32),
            pltpu.VMEM(advanced.shape, jnp.bfloat16),
            pltpu.VMEM((steps, depth, columns * heads // 2), jnp.bfloat16),
            pltpu.VMEM(shape, jnp.bfloat16),
            pltpu.SemaphoreType.DMA((heads + 1,)),
            pltpu.SemaphoreType.DMA((heads // 4,)),
        ],
        compiler_params=pltpu.CompilerParams(vmem_limit_bytes=GRANT),
        cost_estimate=pl.CostEstimate(
            flops=6 * rows * width * heads * dim, bytes_accessed=10 * 2**20, transcendentals=0
        ),
    )(advanced, gain.reshape(1, -1), slices)


def mix_kernel(
    attended_ref, weight_ref, advanced_ref, copied_ref, mixed_ref,
    weight, advanced, mixed, done, sent,
):
    rows, width = advanced.shape
    chunks = weight.shape[0]
    wide = width // chunks
    load_advanced = pltpu.make_async_copy(advanced_ref, advanced, done.at[chunks + 1])
    loads = [
        pltpu.make_async_copy(weight_ref.at[:, b * wide : (b + 1) * wide], weight.at[b], done.at[b])
        for b in range(chunks)
    ]
    for load in (loads[0], load_advanced):
        load.start()
    token_rows = attended_ref[...].T
    for load in loads[1:]:
        load.start()
    stores = []
    for b in range(chunks):
        columns = slice(b * wide, (b + 1) * wide)
        loads[b].wait()
        product = jnp.dot(token_rows, weight[b], preferred_element_type=jnp.float32)
        if b == 0:
            load_advanced.wait()
            stores.append(pltpu.make_async_copy(advanced, copied_ref, sent.at[chunks]))
            stores[-1].start()
        mixed[:, columns] = advanced[:, columns] + product
        stores.append(
            pltpu.make_async_copy(mixed.at[:, columns], mixed_ref.at[:, columns], sent.at[b])
        )
        stores[-1].start()
    for store in stores:
        store.wait()


def mix(attended, weight, advanced):
    depth, rows = attended.shape
    width = advanced.shape[1]
    chunks = width // 256
    far = pl.BlockSpec(memory_space=pl.ANY)
    return pl.pallas_call(
        mix_kernel,
        out_shape=(jax.ShapeDtypeStruct(advanced.shape, jnp.float32),) * 2,
        in_specs=[pl.BlockSpec(memory_space=pltpu.VMEM), far, far],
        out_specs=(far, far),
        scratch_shapes=[
            pltpu.VMEM((chunks, depth, width // chunks), jnp.bfloat16),
            pltpu.VMEM(advanced.shape, jnp.float32),
            pltpu.VMEM(advanced.shape, jnp.float32),
            pltpu.SemaphoreType.DMA((chunks + 2,)),
            pltpu.SemaphoreType.DMA((chunks + 1,)),
        ],
        compiler_params=pltpu.CompilerParams(vmem_limit_bytes=56 * 2**20),
        cost_estimate=pl.CostEstimate(
            flops=2 * rows * depth * width, bytes_accessed=8 * 2**20, transcendentals=0
        ),
    )(attended, weight, advanced)


def swap(blocks, axis):
    return lax.all_to_all(blocks, axis, split_axis=0, concat_axis=0, tiled=True)


def local(states, start, noise, coefficients, context, qkv_weight, out_weights, gain):
    steps, seqs = lax.axis_size("step"), lax.axis_size("seq")
    step, seq = lax.axis_index("step"), lax.axis_index("seq")
    rows, width = start.shape
    tokens, dim = context.shape[1:]

    heads, chips = seqs, seqs // 2
    place = seq.astype(jnp.int32).reshape(1)
    pairs = [(i, i ^ 1) for i in range(seqs)]
    heads_tokens = context[0].T

    first_half, last_shard, *pieces = cut(
        place, heads_tokens, qkv_weight, out_weights, steps, chips
    )
    packed = swap(first_half, "step")

    pieces = [
        lax.ppermute(piece, "seq", [(i, (i + 2 * k + 2) % seqs) for i in range(seqs)])
        for k, piece in enumerate(pieces)
    ]
    kept, given, slices, mine = collect(place, heads_tokens, pieces, packed)
    slices = lax.all_gather(slices, "seq")
    taken = lax.ppermute(given, "seq", pairs)
    other = lax.ppermute(mine, "seq", pairs)
    drift = drift_of(place, coefficients[0], kept, taken, mine, other, states[0], noise[0])

    piece = rows // steps
    drifts = swap(drift.reshape(steps, piece, width), "step")
    advanced = sum_before(drifts, lax.dynamic_slice_in_dim(start, step * piece, piece, 0))
    advanced = swap(advanced, "step").reshape(rows, width)
    by_head = swap(project_qkv(advanced, gain, slices, qkv_weight.shape[0], dim), "seq")
    last_weight = lax.all_gather(last_shard, "step", axis=0, tiled=True)
    attended = swap(attend(by_head), "seq").reshape(seqs * dim, rows)
    advanced, mixed = mix(attended, last_weight, advanced)
    return (advanced[None], mixed[None])


def solution(mesh):
    placed = (
        P("step", "seq", None),
        P("seq", None),
        P("step", "seq", None),
        P("step", None),
        P("step", None, "seq"),
        P("step", None),
        P(None, "step", None),
        P(),
    )
    return jax.shard_map(
        local,
        mesh=mesh,
        in_specs=placed,
        out_specs=(P("step", "seq", None), P("step", "seq", None)),
        check_vma=False,
    )
```

```python
import jax
import jax.numpy as jnp
from jax import lax
from jax.experimental import pallas as pl
from jax.experimental.pallas import tpu as pltpu
from jax.sharding import PartitionSpec as P

HEAD_DIM = 64
GRANT = 60 * 2**20


def attention_kernel(qkv_ref, out_ref, value_rows, scores, tops):
    turn, turns = pl.program_id(0), pl.num_programs(0)
    blocks, _, dim, rows = qkv_ref.shape
    taken = out_ref.shape[0]

    @pl.when(turn == 0)
    def _():
        for j in range(blocks):
            values = qkv_ref[j, 2].astype(jnp.float32)
            padded = jnp.concatenate([values, jnp.ones((dim, rows), jnp.float32)], axis=0)
            value_rows[j * rows : (j + 1) * rows, :] = padded.T.astype(jnp.bfloat16)

    def score(which, slot):
        queries = []
        for b in range(taken):
            query = qkv_ref[which * taken + b, 0].astype(jnp.float32) * (HEAD_DIM**-0.5)
            query = jnp.concatenate([query, query], axis=0).T[:, :dim]
            queries.append(query.astype(jnp.bfloat16))
        queries = jnp.concatenate(queries, axis=0)
        top = None
        for j in range(blocks):
            part = jnp.dot(queries, qkv_ref[j, 1], preferred_element_type=jnp.float32)
            scores[slot, :, j * rows : (j + 1) * rows] = part
            for first in range(0, rows, 128):
                piece = part[:, first : first + 128]
                top = piece if top is None else jnp.maximum(top, piece)
        tops[slot] = jnp.broadcast_to(jnp.max(top, axis=-1, keepdims=True), top.shape)

    def finish(slot):
        top = tops[slot][:, :1]
        total = jnp.zeros((taken * rows, 2 * dim), jnp.float32)
        for j in range(blocks):
            keys = slice(j * rows, (j + 1) * rows)
            weights = jnp.exp(scores[slot, :, keys] - top).astype(jnp.bfloat16)
            total = total + jnp.dot(weights, value_rows[keys, :], preferred_element_type=jnp.float32)
        total = total.T
        attended = (total[:dim] / total[dim:]).astype(jnp.bfloat16)
        for b in range(taken):
            out_ref[b] = attended[:, b * rows : (b + 1) * rows]

    @pl.when(turn == 0)
    def _():
        score(0, 0)

    for slot in (0, 1):

        @pl.when((lax.rem(turn, 2) == slot) & (turn < turns - 1))
        def _():
            score(turn + 1, 1 - slot)
            finish(slot)

        @pl.when((lax.rem(turn, 2) == slot) & (turn == turns - 1))
        def _():
            finish(slot)


def attend(qkv):
    blocks, _, dim, rows = qkv.shape
    taken = 4
    return pl.pallas_call(
        attention_kernel,
        out_shape=jax.ShapeDtypeStruct((blocks, dim, rows), jnp.bfloat16),
        grid=(blocks // taken,),
        in_specs=[pl.BlockSpec(qkv.shape, lambda i: (0, 0, 0, 0))],
        out_specs=pl.BlockSpec((taken, dim, rows), lambda i: (i, 0, 0)),
        scratch_shapes=[
            pltpu.VMEM((blocks * rows, 2 * dim), jnp.bfloat16),
            pltpu.VMEM((2, taken * rows, blocks * rows), jnp.float32),
            pltpu.VMEM((2, taken * rows, 128), jnp.float32),
        ],
        compiler_params=pltpu.CompilerParams(
            dimension_semantics=("arbitrary",), vmem_limit_bytes=48 * 2**20
        ),
        cost_estimate=pl.CostEstimate(
            flops=16 * 2**30, bytes_accessed=3 * 2**20, transcendentals=2**24
        ),
    )(qkv)


def position(seq_ref):
    return lax.rem(seq_ref[0], 2), lax.div(seq_ref[0], 2)


def tiles(count):
    for n in range(3 * count):
        yield slice(16 * (n // 3), 16 * (n // 3) + 16), 128 * (n % 3), 16 * (n // 5), 128 * (n % 5)


def pack_kernel(seq_ref, qkv_ref, weights_ref, packed_ref, shard, done, sent):
    core, chip = position(seq_ref)
    depth, half = weights_ref.shape[1], packed_ref.shape[2]
    inner = qkv_ref.shape[1] // 3
    shard[depth:, :] = jnp.zeros((shard.shape[0] - depth, half), jnp.bfloat16)
    loads = [
        pltpu.make_async_copy(
            weights_ref.at[0, :, pl.ds(pl.multiple_of(core * half, half), half)],
            shard.at[:depth],
            done.at[0],
        )
    ]
    for n, (rows, column, low, left) in enumerate(tiles(3)):
        first_row = pl.multiple_of(32 * core + rows.start, 16)
        first_column = pl.multiple_of(column // 128 * inner + 128 * chip, 128)
        loads.append(
            pltpu.make_async_copy(
                qkv_ref.at[pl.ds(first_row, 16), pl.ds(first_column, 128)],
                shard.at[depth + low : depth + low + 16, left : left + 128],
                done.at[1 + n],
            )
        )
    for load in loads:
        load.start()
    for load in loads:
        load.wait()
    stores = []
    for i in range(packed_ref.shape[0]):
        stores.append(pltpu.make_async_copy(shard, packed_ref.at[i], sent.at[i]))
        stores[-1].start()
    for store in stores:
        store.wait()


def pack(seq, qkv_weight, out_weights, steps):
    _, depth, width = out_weights.shape
    shape = (steps, depth + 32, width // 2)
    far = pl.BlockSpec(memory_space=pl.ANY)
    return pl.pallas_call(
        pack_kernel,
        out_shape=jax.ShapeDtypeStruct(shape, jnp.bfloat16),
        in_specs=[pl.BlockSpec(memory_space=pltpu.SMEM)] + [far] * 2,
        out_specs=far,
        scratch_shapes=[
            pltpu.VMEM(shape[1:], jnp.bfloat16),
            pltpu.SemaphoreType.DMA((10,)),
            pltpu.SemaphoreType.DMA((steps,)),
        ],
        compiler_params=pltpu.CompilerParams(vmem_limit_bytes=GRANT),
        cost_estimate=pl.CostEstimate(flops=0, bytes_accessed=2 * 2**20, transcendentals=0),
    )(seq, qkv_weight, out_weights)


def cut_kernel(seq_ref, context_ref, weights_ref, last_ref, *refs):
    *pieces, context, last, done, sent = refs
    _, chip = position(seq_ref)
    chips = len(pieces) + 1
    width = pieces[0].shape[1]
    load_context = pltpu.make_async_copy(context_ref, context, done.at[0])
    load_last = pltpu.make_async_copy(weights_ref.at[1], last, done.at[1])
    load_context.start()
    load_last.start()
    load_context.wait()
    stores = []
    for k, piece in enumerate(pieces):
        target = lax.rem(chip + k + 1, chips)
        tokens = pl.ds(pl.multiple_of(target * width, width), width)
        stores.append(pltpu.make_async_copy(context.at[:, tokens], piece, sent.at[k]))
        stores[-1].start()
    load_last.wait()
    stores.append(pltpu.make_async_copy(last, last_ref, sent.at[chips - 1]))
    stores[-1].start()
    for store in stores:
        store.wait()


def cut(seq, context, out_weights, chips):
    dim, tokens = context.shape
    _, depth, width = out_weights.shape
    far = pl.BlockSpec(memory_space=pl.ANY)
    shapes = [(depth, width)] + [(dim, tokens // chips)] * (chips - 1)
    return pl.pallas_call(
        cut_kernel,
        out_shape=[jax.ShapeDtypeStruct(shape, jnp.bfloat16) for shape in shapes],
        in_specs=[pl.BlockSpec(memory_space=pltpu.SMEM)] + [far] * 2,
        out_specs=[far] * len(shapes),
        scratch_shapes=[
            pltpu.VMEM(context.shape, jnp.bfloat16),
            pltpu.VMEM(shapes[0], jnp.bfloat16),
            pltpu.SemaphoreType.DMA((2,)),
            pltpu.SemaphoreType.DMA((chips,)),
        ],
        compiler_params=pltpu.CompilerParams(vmem_limit_bytes=GRANT),
        cost_estimate=pl.CostEstimate(flops=0, bytes_accessed=2 * 2**20, transcendentals=0),
    )(seq, context, out_weights)


def collect_kernel(seq_ref, context_ref, *refs):
    *pieces, packed_ref, kept_ref, given_ref, slices_ref, _, arrived, slices, done, sent = refs
    core, chip = position(seq_ref)
    chips = len(pieces) + 1
    rows = kept_ref.shape[2]
    depth = packed_ref.shape[1] - 32
    own = context_ref.at[:, pl.ds(pl.multiple_of(2 * rows * chip, 2 * rows), 2 * rows)]
    loads = []
    for k, piece in enumerate((own, *pieces)):
        source = lax.rem(chip - k + chips, chips)
        loads.append(pltpu.make_async_copy(piece, arrived.at[source], done.at[9 + k]))
        loads[-1].start()
    unpacks = []
    for n, (place, column, low, left) in enumerate(tiles(3)):
        unpacks.append(
            pltpu.make_async_copy(
                packed_ref.at[:, depth + low : depth + low + 16, left : left + 128],
                slices.at[:, place, column : column + 128],
                done.at[n],
            )
        )
        unpacks[-1].start()
    for load in loads:
        load.wait()
    stores = []
    for turn, (side, out_ref) in enumerate(((1 - core, given_ref), (core, kept_ref))):
        tokens = pl.ds(pl.multiple_of(side * rows, rows), rows)
        stores.append(pltpu.make_async_copy(arrived.at[:, :, tokens], out_ref, sent.at[turn]))
        stores[-1].start()
    for unpack in unpacks:
        unpack.wait()
    stores.append(pltpu.make_async_copy(slices, slices_ref, sent.at[2]))
    stores[-1].start()
    for store in stores:
        store.wait()


def collect(seq, context, pieces, packed):
    dim, width = pieces[0].shape
    chips = len(pieces) + 1
    shape = (packed.shape[0], 48, 384)
    far = pl.BlockSpec(memory_space=pl.ANY)
    return pl.pallas_call(
        collect_kernel,
        out_shape=(jax.ShapeDtypeStruct((chips, dim, width // 2), jnp.bfloat16),) * 2
        + (
            jax.ShapeDtypeStruct(shape, jnp.bfloat16),
            jax.ShapeDtypeStruct(packed.shape, jnp.bfloat16),
        ),
        in_specs=[pl.BlockSpec(memory_space=pltpu.SMEM)] + [far] * (chips + 1),
        out_specs=(far,) * 4,
        input_output_aliases={chips + 1: 3},
        scratch_shapes=[
            pltpu.VMEM((chips, dim, width), jnp.bfloat16),
            pltpu.VMEM(shape, jnp.bfloat16),
            pltpu.SemaphoreType.DMA((9 + chips,)),
            pltpu.SemaphoreType.DMA((3,)),
        ],
        compiler_params=pltpu.CompilerParams(vmem_limit_bytes=GRANT),
        cost_estimate=pl.CostEstimate(flops=0, bytes_accessed=2**20, transcendentals=0),
    )(seq, context, *pieces, packed)


def drift_kernel(
    seq_ref, factors_ref, kept_ref, taken_ref, mine_ref, other_ref, states_ref, noise_ref,
    drift_ref, context, weights, states, noise, drift, done,
):
    core, _ = position(seq_ref)
    chips, _, dim, rows = context.shape
    half = weights.shape[3]
    loads = [
        pltpu.make_async_copy(kept_ref, context.at[:, core], done.at[0]),
        pltpu.make_async_copy(taken_ref, context.at[:, 1 - core], done.at[1]),
        pltpu.make_async_copy(mine_ref.at[:, :dim, :], weights.at[0], done.at[2]),
        pltpu.make_async_copy(other_ref.at[:, :dim, :], weights.at[1], done.at[3]),
        pltpu.make_async_copy(states_ref, states, done.at[4]),
        pltpu.make_async_copy(noise_ref, noise, done.at[5]),
    ]
    for load in loads:
        load.start()
    loads[0].wait()
    loads[1].wait()
    token_rows = context[...].reshape(chips * 2 * dim, rows).T
    stores = []
    for turn, side in enumerate((core, 1 - core)):
        loads[2 + turn].wait()
        weight = weights[turn].reshape(chips * 2 * dim, half)
        product = jnp.dot(token_rows, weight, preferred_element_type=jnp.float32)
        if turn == 0:
            loads[4].wait()
            loads[5].wait()
        columns = pl.ds(pl.multiple_of(side * half, half), half)
        drift[:, columns] = (
            (factors_ref[0] + factors_ref[1]) * states[:, columns]
            + factors_ref[1] * product
            + factors_ref[2] * noise[:, columns].astype(jnp.float32)
        )
        stores.append(
            pltpu.make_async_copy(drift.at[:, columns], drift_ref.at[:, columns], done.at[6 + turn])
        )
        stores[-1].start()
    for store in stores:
        store.wait()


def drift_of(seq, factors, kept, taken, mine, other, states, noise):
    chips, dim, rows = kept.shape
    scalars = pl.BlockSpec(memory_space=pltpu.SMEM)
    far = pl.BlockSpec(memory_space=pl.ANY)
    return pl.pallas_call(
        drift_kernel,
        out_shape=jax.ShapeDtypeStruct(states.shape, jnp.float32),
        in_specs=[scalars] * 2 + [far] * 6,
        out_specs=far,
        scratch_shapes=[
            pltpu.VMEM((chips, 2, dim, rows), jnp.bfloat16),
            pltpu.VMEM((2, mine.shape[0], dim, mine.shape[2]), jnp.bfloat16),
            pltpu.VMEM(states.shape, jnp.float32),
            pltpu.VMEM(states.shape, jnp.bfloat16),
            pltpu.VMEM(states.shape, jnp.float32),
            pltpu.SemaphoreType.DMA((8,)),
        ],
        compiler_params=pltpu.CompilerParams(vmem_limit_bytes=GRANT),
        cost_estimate=pl.CostEstimate(
            flops=2**11 * states.size, bytes_accessed=8 * 2**20, transcendentals=0
        ),
    )(seq, factors, kept, taken, mine, other, states, noise)


def sum_kernel(drifts_ref, start_ref, advanced_ref):
    running = start_ref[...]
    for j in range(drifts_ref.shape[0]):
        advanced_ref[j] = running
        running = running + drifts_ref[j]


def sum_before(drifts, start):
    whole = pl.BlockSpec(memory_space=pltpu.VMEM)
    return pl.pallas_call(
        sum_kernel,
        out_shape=jax.ShapeDtypeStruct(drifts.shape, jnp.float32),
        in_specs=[whole] * 2,
        out_specs=whole,
        compiler_params=pltpu.CompilerParams(vmem_limit_bytes=16 * 2**20),
        cost_estimate=pl.CostEstimate(
            flops=drifts.size, bytes_accessed=8 * drifts.size, transcendentals=0
        ),
    )(drifts, start)


def qkv_kernel(
    advanced_ref, gain_ref, slices_ref, out_ref, advanced, normed, weights, projected, done, sent
):
    _, _, dim, rows = out_ref.shape
    chips = slices_ref.shape[0] // 2
    steps, depth, _ = weights.shape
    columns, upper = slices_ref.shape[3], slices_ref.shape[2]
    load_rows = pltpu.make_async_copy(advanced_ref, advanced, done.at[2 * chips])
    load_rows.start()
    loads = []
    for c in range(chips):
        place = slice(c * columns, (c + 1) * columns)
        rest = depth - upper
        loads.append(
            (
                pltpu.make_async_copy(
                    slices_ref.at[2 * c], weights.at[:, :upper, place], done.at[2 * c]
                ),
                pltpu.make_async_copy(
                    slices_ref.at[2 * c + 1, :, upper - rest :],
                    weights.at[:, upper:, place],
                    done.at[2 * c + 1],
                ),
            )
        )
    for pair in loads[:2]:
        for load in pair:
            load.start()
    load_rows.wait()
    for pair in loads[2:4]:
        for load in pair:
            load.start()
    gain = gain_ref[...]
    part_rows = 32
    for first in range(0, rows, part_rows):
        some = advanced[first : first + part_rows, :]
        mean = jnp.mean(some, axis=-1, keepdims=True)
        centred = some - mean
        variance = jnp.mean(centred * centred, axis=-1, keepdims=True)
        normed[first : first + part_rows, :] = (
            centred * lax.rsqrt(variance + 1e-05) * gain
        ).astype(jnp.bfloat16)
    stores = []
    for c in range(0, chips, 2):
        for pair in loads[c : c + 2]:
            for load in pair:
                load.wait()
        for pair in loads[c + 4 : c + 6]:
            for load in pair:
                load.start()
        weight = weights[:, :, c * columns : (c + 2) * columns].reshape(steps * depth, 2 * columns)
        part = jnp.dot(normed[...], weight, preferred_element_type=jnp.float32)
        part = part.T.astype(jnp.bfloat16).reshape(2, 3, 2, dim, rows)
        for b in (0, 1):
            for kind in range(3):
                projected[2 * (c + b) : 2 * (c + b) + 2, kind] = part[b, kind]
        heads = slice(2 * c, 2 * c + 4)
        stores.append(
            pltpu.make_async_copy(projected.at[heads], out_ref.at[heads], sent.at[c // 2])
        )
        stores[-1].start()
    for store in stores:
        store.wait()


def project_qkv(advanced, gain, slices, depth, dim):
    rows, width = advanced.shape
    heads, steps, _, columns = slices.shape
    shape = (heads, 3, dim, rows)
    far = pl.BlockSpec(memory_space=pl.ANY)
    return pl.pallas_call(
        qkv_kernel,
        out_shape=jax.ShapeDtypeStruct(shape, jnp.bfloat16),
        in_specs=[far, pl.BlockSpec(memory_space=pltpu.VMEM), far],
        out_specs=far,
        scratch_shapes=[
            pltpu.VMEM(advanced.shape, jnp.float32),
            pltpu.VMEM(advanced.shape, jnp.bfloat16),
            pltpu.VMEM((steps, depth, columns * heads // 2), jnp.bfloat16),
            pltpu.VMEM(shape, jnp.bfloat16),
            pltpu.SemaphoreType.DMA((heads + 1,)),
            pltpu.SemaphoreType.DMA((heads // 4,)),
        ],
        compiler_params=pltpu.CompilerParams(vmem_limit_bytes=GRANT),
        cost_estimate=pl.CostEstimate(
            flops=6 * rows * width * heads * dim, bytes_accessed=10 * 2**20, transcendentals=0
        ),
    )(advanced, gain.reshape(1, -1), slices)


def mix_kernel(
    attended_ref, weight_ref, advanced_ref, copied_ref, mixed_ref,
    weight, advanced, mixed, done, sent,
):
    rows, width = advanced.shape
    chunks = weight.shape[0]
    wide = width // chunks
    load_advanced = pltpu.make_async_copy(advanced_ref, advanced, done.at[chunks + 1])
    loads = [
        pltpu.make_async_copy(weight_ref.at[:, b * wide : (b + 1) * wide], weight.at[b], done.at[b])
        for b in range(chunks)
    ]
    for load in (loads[0], load_advanced):
        load.start()
    token_rows = attended_ref[...].T
    for load in loads[1:]:
        load.start()
    stores = []
    for b in range(chunks):
        columns = slice(b * wide, (b + 1) * wide)
        loads[b].wait()
        product = jnp.dot(token_rows, weight[b], preferred_element_type=jnp.float32)
        if b == 0:
            load_advanced.wait()
            stores.append(pltpu.make_async_copy(advanced, copied_ref, sent.at[chunks]))
            stores[-1].start()
        mixed[:, columns] = advanced[:, columns] + product
        stores.append(
            pltpu.make_async_copy(mixed.at[:, columns], mixed_ref.at[:, columns], sent.at[b])
        )
        stores[-1].start()
    for store in stores:
        store.wait()


def mix(attended, weight, advanced):
    depth, rows = attended.shape
    width = advanced.shape[1]
    chunks = width // 256
    far = pl.BlockSpec(memory_space=pl.ANY)
    return pl.pallas_call(
        mix_kernel,
        out_shape=(jax.ShapeDtypeStruct(advanced.shape, jnp.float32),) * 2,
        in_specs=[pl.BlockSpec(memory_space=pltpu.VMEM), far, far],
        out_specs=(far, far),
        scratch_shapes=[
            pltpu.VMEM((chunks, depth, width // chunks), jnp.bfloat16),
            pltpu.VMEM(advanced.shape, jnp.float32),
            pltpu.VMEM(advanced.shape, jnp.float32),
            pltpu.SemaphoreType.DMA((chunks + 2,)),
            pltpu.SemaphoreType.DMA((chunks + 1,)),
        ],
        compiler_params=pltpu.CompilerParams(vmem_limit_bytes=56 * 2**20),
        cost_estimate=pl.CostEstimate(
            flops=2 * rows * depth * width, bytes_accessed=8 * 2**20, transcendentals=0
        ),
    )(attended, weight, advanced)


def swap(blocks, axis):
    return lax.all_to_all(blocks, axis, split_axis=0, concat_axis=0, tiled=True)


def local(states, start, noise, coefficients, context, qkv_weight, out_weights, gain):
    steps, seqs = lax.axis_size("step"), lax.axis_size("seq")
    step, seq = lax.axis_index("step"), lax.axis_index("seq")
    rows, width = start.shape
    tokens, dim = context.shape[1:]

    heads, chips = seqs, seqs // 2
    place = seq.astype(jnp.int32).reshape(1)
    pairs = [(i, i ^ 1) for i in range(seqs)]
    heads_tokens = context[0].T

    packed = swap(pack(place, qkv_weight, out_weights, steps), "step")
    last_shard, *pieces = cut(place, heads_tokens, out_weights, chips)

    pieces = [
        lax.ppermute(piece, "seq", [(i, (i + 2 * k + 2) % seqs) for i in range(seqs)])
        for k, piece in enumerate(pieces)
    ]
    kept, given, slices, mine = collect(place, heads_tokens, pieces, packed)
    slices = lax.all_gather(slices, "seq")
    taken = lax.ppermute(given, "seq", pairs)
    other = lax.ppermute(mine, "seq", pairs)
    drift = drift_of(place, coefficients[0], kept, taken, mine, other, states[0], noise[0])

    piece = rows // steps
    drifts = swap(drift.reshape(steps, piece, width), "step")
    advanced = sum_before(drifts, lax.dynamic_slice_in_dim(start, step * piece, piece, 0))
    advanced = swap(advanced, "step").reshape(rows, width)
    by_head = swap(project_qkv(advanced, gain, slices, qkv_weight.shape[0], dim), "seq")
    last_weight = lax.all_gather(last_shard, "step", axis=0, tiled=True)
    attended = swap(attend(by_head), "seq").reshape(seqs * dim, rows)
    advanced, mixed = mix(attended, last_weight, advanced)
    return (advanced[None], mixed[None])


def solution(mesh):
    placed = (
        P("step", "seq", None),
        P("seq", None),
        P("step", "seq", None),
        P("step", None),
        P("step", None, "seq"),
        P("step", None),
        P(None, "step", None),
        P(),
    )
    return jax.shard_map(
        local,
        mesh=mesh,
        in_specs=placed,
        out_specs=(P("step", "seq", None), P("step", "seq", None)),
        check_vma=False,
    )
```

```python
import jax
import jax.numpy as jnp
from jax import lax
from jax.experimental import pallas as pl
from jax.experimental.pallas import tpu as pltpu
from jax.sharding import PartitionSpec as P

HEAD_DIM = 64
GRANT = 60 * 2**20


def attention_kernel(qkv_ref, out_ref, value_rows, scores, tops):
    turn, turns = pl.program_id(0), pl.num_programs(0)
    blocks, _, dim, rows = qkv_ref.shape
    taken = out_ref.shape[0]

    @pl.when(turn == 0)
    def _():
        for j in range(blocks):
            values = qkv_ref[j, 2].astype(jnp.float32)
            padded = jnp.concatenate([values, jnp.ones((dim, rows), jnp.float32)], axis=0)
            value_rows[j * rows : (j + 1) * rows, :] = padded.T.astype(jnp.bfloat16)

    def score(which, slot):
        queries = []
        for b in range(taken):
            query = qkv_ref[which * taken + b, 0].astype(jnp.float32) * (HEAD_DIM**-0.5)
            query = jnp.concatenate([query, query], axis=0).T[:, :dim]
            queries.append(query.astype(jnp.bfloat16))
        queries = jnp.concatenate(queries, axis=0)
        top = None
        for j in range(blocks):
            part = jnp.dot(queries, qkv_ref[j, 1], preferred_element_type=jnp.float32)
            scores[slot, :, j * rows : (j + 1) * rows] = part
            for first in range(0, rows, 128):
                piece = part[:, first : first + 128]
                top = piece if top is None else jnp.maximum(top, piece)
        tops[slot] = jnp.broadcast_to(jnp.max(top, axis=-1, keepdims=True), top.shape)

    def finish(slot):
        top = tops[slot][:, :1]
        total = jnp.zeros((taken * rows, 2 * dim), jnp.float32)
        for j in range(blocks):
            keys = slice(j * rows, (j + 1) * rows)
            weights = jnp.exp(scores[slot, :, keys] - top).astype(jnp.bfloat16)
            total = total + jnp.dot(weights, value_rows[keys, :], preferred_element_type=jnp.float32)
        total = total.T
        attended = (total[:dim] / total[dim:]).astype(jnp.bfloat16)
        for b in range(taken):
            out_ref[b] = attended[:, b * rows : (b + 1) * rows]

    @pl.when(turn == 0)
    def _():
        score(0, 0)

    for slot in (0, 1):

        @pl.when((lax.rem(turn, 2) == slot) & (turn < turns - 1))
        def _():
            score(turn + 1, 1 - slot)
            finish(slot)

        @pl.when((lax.rem(turn, 2) == slot) & (turn == turns - 1))
        def _():
            finish(slot)


def attend(qkv):
    blocks, _, dim, rows = qkv.shape
    taken = 4
    return pl.pallas_call(
        attention_kernel,
        out_shape=jax.ShapeDtypeStruct((blocks, dim, rows), jnp.bfloat16),
        grid=(blocks // taken,),
        in_specs=[pl.BlockSpec(qkv.shape, lambda i: (0, 0, 0, 0))],
        out_specs=pl.BlockSpec((taken, dim, rows), lambda i: (i, 0, 0)),
        scratch_shapes=[
            pltpu.VMEM((blocks * rows, 2 * dim), jnp.bfloat16),
            pltpu.VMEM((2, taken * rows, blocks * rows), jnp.float32),
            pltpu.VMEM((2, taken * rows, 128), jnp.float32),
        ],
        compiler_params=pltpu.CompilerParams(
            dimension_semantics=("arbitrary",), vmem_limit_bytes=48 * 2**20
        ),
        cost_estimate=pl.CostEstimate(
            flops=16 * 2**30, bytes_accessed=3 * 2**20, transcendentals=2**24
        ),
    )(qkv)


def position(seq_ref):
    return lax.rem(seq_ref[0], 2), lax.div(seq_ref[0], 2)


def tiles(count):
    for n in range(3 * count):
        yield slice(16 * (n // 3), 16 * (n // 3) + 16), 128 * (n % 3), 16 * (n // 5), 128 * (n % 5)


def cut_kernel(seq_ref, context_ref, qkv_ref, weights_ref, first_ref, last_ref, *refs):
    *pieces, context, shard, last, done, sent = refs
    core, chip = position(seq_ref)
    chips = len(pieces) + 1
    depth, half, width = weights_ref.shape[1], first_ref.shape[2], pieces[0].shape[1]
    inner = qkv_ref.shape[1] // 3
    shard[depth:, :] = jnp.zeros((shard.shape[0] - depth, half), jnp.bfloat16)
    loads = [
        pltpu.make_async_copy(
            weights_ref.at[0, :, pl.ds(pl.multiple_of(core * half, half), half)],
            shard.at[:depth],
            done.at[0],
        )
    ]
    for n, (rows, column, low, left) in enumerate(tiles(3)):
        first_row = pl.multiple_of(32 * core + rows.start, 16)
        first_column = pl.multiple_of(column // 128 * inner + 128 * chip, 128)
        loads.append(
            pltpu.make_async_copy(
                qkv_ref.at[pl.ds(first_row, 16), pl.ds(first_column, 128)],
                shard.at[depth + low : depth + low + 16, left : left + 128],
                done.at[3 + n],
            )
        )
    load_context = pltpu.make_async_copy(context_ref, context, done.at[1])
    load_last = pltpu.make_async_copy(weights_ref.at[1], last, done.at[2])
    for load in (*loads, load_context, load_last):
        load.start()
    for load in loads:
        load.wait()
    stores = []
    for i in range(first_ref.shape[0]):
        stores.append(pltpu.make_async_copy(shard, first_ref.at[i], sent.at[chips + i]))
        stores[-1].start()
    load_context.wait()
    for k, piece in enumerate(pieces):
        target = lax.rem(chip + k + 1, chips)
        tokens = pl.ds(pl.multiple_of(target * width, width), width)
        stores.append(pltpu.make_async_copy(context.at[:, tokens], piece, sent.at[k]))
        stores[-1].start()
    load_last.wait()
    stores.append(pltpu.make_async_copy(last, last_ref, sent.at[chips - 1]))
    stores[-1].start()
    for store in stores:
        store.wait()


def cut(seq, context, qkv_weight, out_weights, steps, chips):
    dim, tokens = context.shape
    _, depth, width = out_weights.shape
    far = pl.BlockSpec(memory_space=pl.ANY)
    shapes = [(steps, depth + 32, width // 2), (depth, width)] + [(dim, tokens // chips)] * (chips - 1)
    return pl.pallas_call(
        cut_kernel,
        out_shape=[jax.ShapeDtypeStruct(shape, jnp.bfloat16) for shape in shapes],
        in_specs=[pl.BlockSpec(memory_space=pltpu.SMEM)] + [far] * 3,
        out_specs=[far] * len(shapes),
        scratch_shapes=[
            pltpu.VMEM(context.shape, jnp.bfloat16),
            pltpu.VMEM(shapes[0][1:], jnp.bfloat16),
            pltpu.VMEM(shapes[1], jnp.bfloat16),
            pltpu.SemaphoreType.DMA((12,)),
            pltpu.SemaphoreType.DMA((chips + steps,)),
        ],
        compiler_params=pltpu.CompilerParams(vmem_limit_bytes=GRANT),
        cost_estimate=pl.CostEstimate(flops=0, bytes_accessed=4 * 2**20, transcendentals=0),
    )(seq, context, qkv_weight, out_weights)


def collect_kernel(seq_ref, context_ref, *refs):
    *pieces, packed_ref, kept_ref, given_ref, slices_ref, _, arrived, slices, done, sent = refs
    core, chip = position(seq_ref)
    chips = len(pieces) + 1
    rows = kept_ref.shape[2]
    depth = packed_ref.shape[1] - 32
    own = context_ref.at[:, pl.ds(pl.multiple_of(2 * rows * chip, 2 * rows), 2 * rows)]
    loads = []
    for k, piece in enumerate((own, *pieces)):
        source = lax.rem(chip - k + chips, chips)
        loads.append(pltpu.make_async_copy(piece, arrived.at[source], done.at[9 + k]))
        loads[-1].start()
    unpacks = []
    for n, (place, column, low, left) in enumerate(tiles(3)):
        unpacks.append(
            pltpu.make_async_copy(
                packed_ref.at[:, depth + low : depth + low + 16, left : left + 128],
                slices.at[:, place, column : column + 128],
                done.at[n],
            )
        )
        unpacks[-1].start()
    for load in loads:
        load.wait()
    stores = []
    for turn, (side, out_ref) in enumerate(((1 - core, given_ref), (core, kept_ref))):
        tokens = pl.ds(pl.multiple_of(side * rows, rows), rows)
        stores.append(pltpu.make_async_copy(arrived.at[:, :, tokens], out_ref, sent.at[turn]))
        stores[-1].start()
    for unpack in unpacks:
        unpack.wait()
    stores.append(pltpu.make_async_copy(slices, slices_ref, sent.at[2]))
    stores[-1].start()
    for store in stores:
        store.wait()


def collect(seq, context, pieces, packed):
    dim, width = pieces[0].shape
    chips = len(pieces) + 1
    shape = (packed.shape[0], 48, 384)
    far = pl.BlockSpec(memory_space=pl.ANY)
    return pl.pallas_call(
        collect_kernel,
        out_shape=(jax.ShapeDtypeStruct((chips, dim, width // 2), jnp.bfloat16),) * 2
        + (
            jax.ShapeDtypeStruct(shape, jnp.bfloat16),
            jax.ShapeDtypeStruct(packed.shape, jnp.bfloat16),
        ),
        in_specs=[pl.BlockSpec(memory_space=pltpu.SMEM)] + [far] * (chips + 1),
        out_specs=(far,) * 4,
        input_output_aliases={chips + 1: 3},
        scratch_shapes=[
            pltpu.VMEM((chips, dim, width), jnp.bfloat16),
            pltpu.VMEM(shape, jnp.bfloat16),
            pltpu.SemaphoreType.DMA((9 + chips,)),
            pltpu.SemaphoreType.DMA((3,)),
        ],
        compiler_params=pltpu.CompilerParams(vmem_limit_bytes=GRANT),
        cost_estimate=pl.CostEstimate(flops=0, bytes_accessed=2**20, transcendentals=0),
    )(seq, context, *pieces, packed)


def drift_kernel(
    seq_ref, factors_ref, kept_ref, taken_ref, mine_ref, other_ref, states_ref, noise_ref,
    drift_ref, context, weights, states, noise, drift, done,
):
    core, _ = position(seq_ref)
    chips, _, dim, rows = context.shape
    half = weights.shape[3]
    loads = [
        pltpu.make_async_copy(kept_ref, context.at[:, core], done.at[0]),
        pltpu.make_async_copy(taken_ref, context.at[:, 1 - core], done.at[1]),
        pltpu.make_async_copy(mine_ref.at[:, :dim, :], weights.at[0], done.at[2]),
        pltpu.make_async_copy(other_ref.at[:, :dim, :], weights.at[1], done.at[3]),
        pltpu.make_async_copy(states_ref, states, done.at[4]),
        pltpu.make_async_copy(noise_ref, noise, done.at[5]),
    ]
    for load in loads:
        load.start()
    loads[0].wait()
    loads[1].wait()
    token_rows = context[...].reshape(chips * 2 * dim, rows).T
    stores = []
    for turn, side in enumerate((core, 1 - core)):
        loads[2 + turn].wait()
        weight = weights[turn].reshape(chips * 2 * dim, half)
        product = jnp.dot(token_rows, weight, preferred_element_type=jnp.float32)
        if turn == 0:
            loads[4].wait()
            loads[5].wait()
        columns = pl.ds(pl.multiple_of(side * half, half), half)
        drift[:, columns] = (
            (factors_ref[0] + factors_ref[1]) * states[:, columns]
            + factors_ref[1] * product
            + factors_ref[2] * noise[:, columns].astype(jnp.float32)
        )
        stores.append(
            pltpu.make_async_copy(drift.at[:, columns], drift_ref.at[:, columns], done.at[6 + turn])
        )
        stores[-1].start()
    for store in stores:
        store.wait()


def drift_of(seq, factors, kept, taken, mine, other, states, noise):
    chips, dim, rows = kept.shape
    scalars = pl.BlockSpec(memory_space=pltpu.SMEM)
    far = pl.BlockSpec(memory_space=pl.ANY)
    return pl.pallas_call(
        drift_kernel,
        out_shape=jax.ShapeDtypeStruct(states.shape, jnp.float32),
        in_specs=[scalars] * 2 + [far] * 6,
        out_specs=far,
        scratch_shapes=[
            pltpu.VMEM((chips, 2, dim, rows), jnp.bfloat16),
            pltpu.VMEM((2, mine.shape[0], dim, mine.shape[2]), jnp.bfloat16),
            pltpu.VMEM(states.shape, jnp.float32),
            pltpu.VMEM(states.shape, jnp.bfloat16),
            pltpu.VMEM(states.shape, jnp.float32),
            pltpu.SemaphoreType.DMA((8,)),
        ],
        compiler_params=pltpu.CompilerParams(vmem_limit_bytes=GRANT),
        cost_estimate=pl.CostEstimate(
            flops=2**11 * states.size, bytes_accessed=8 * 2**20, transcendentals=0
        ),
    )(seq, factors, kept, taken, mine, other, states, noise)


def sum_kernel(drifts_ref, start_ref, advanced_ref):
    running = start_ref[...]
    for j in range(drifts_ref.shape[0]):
        advanced_ref[j] = running
        running = running + drifts_ref[j]


def sum_before(drifts, start):
    whole = pl.BlockSpec(memory_space=pltpu.VMEM)
    return pl.pallas_call(
        sum_kernel,
        out_shape=jax.ShapeDtypeStruct(drifts.shape, jnp.float32),
        in_specs=[whole] * 2,
        out_specs=whole,
        compiler_params=pltpu.CompilerParams(vmem_limit_bytes=16 * 2**20),
        cost_estimate=pl.CostEstimate(
            flops=drifts.size, bytes_accessed=8 * drifts.size, transcendentals=0
        ),
    )(drifts, start)


def qkv_kernel(
    advanced_ref, gain_ref, slices_ref, out_ref, advanced, normed, weights, projected, done, sent
):
    _, _, dim, rows = out_ref.shape
    chips = slices_ref.shape[0] // 2
    steps, depth, _ = weights.shape
    columns, upper = slices_ref.shape[3], slices_ref.shape[2]
    load_rows = pltpu.make_async_copy(advanced_ref, advanced, done.at[2 * chips])
    load_rows.start()
    loads = []
    for c in range(chips):
        place = slice(c * columns, (c + 1) * columns)
        rest = depth - upper
        loads.append(
            (
                pltpu.make_async_copy(
                    slices_ref.at[2 * c], weights.at[:, :upper, place], done.at[2 * c]
                ),
                pltpu.make_async_copy(
                    slices_ref.at[2 * c + 1, :, upper - rest :],
                    weights.at[:, upper:, place],
                    done.at[2 * c + 1],
                ),
            )
        )
    for pair in loads[:2]:
        for load in pair:
            load.start()
    load_rows.wait()
    for pair in loads[2:4]:
        for load in pair:
            load.start()
    gain = gain_ref[...]
    part_rows = 32
    for first in range(0, rows, part_rows):
        some = advanced[first : first + part_rows, :]
        mean = jnp.mean(some, axis=-1, keepdims=True)
        centred = some - mean
        variance = jnp.mean(centred * centred, axis=-1, keepdims=True)
        normed[first : first + part_rows, :] = (
            centred * lax.rsqrt(variance + 1e-05) * gain
        ).astype(jnp.bfloat16)
    stores = []
    for c in range(0, chips, 2):
        for pair in loads[c : c + 2]:
            for load in pair:
                load.wait()
        for pair in loads[c + 4 : c + 6]:
            for load in pair:
                load.start()
        weight = weights[:, :, c * columns : (c + 2) * columns].reshape(steps * depth, 2 * columns)
        part = jnp.dot(normed[...], weight, preferred_element_type=jnp.float32)
        part = part.T.astype(jnp.bfloat16).reshape(2, 3, 2, dim, rows)
        for b in (0, 1):
            for kind in range(3):
                projected[2 * (c + b) : 2 * (c + b) + 2, kind] = part[b, kind]
        heads = slice(2 * c, 2 * c + 4)
        stores.append(
            pltpu.make_async_copy(projected.at[heads], out_ref.at[heads], sent.at[c // 2])
        )
        stores[-1].start()
    for store in stores:
        store.wait()


def project_qkv(advanced, gain, slices, depth, dim):
    rows, width = advanced.shape
    heads, steps, _, columns = slices.shape
    shape = (heads, 3, dim, rows)
    far = pl.BlockSpec(memory_space=pl.ANY)
    return pl.pallas_call(
        qkv_kernel,
        out_shape=jax.ShapeDtypeStruct(shape, jnp.bfloat16),
        in_specs=[far, pl.BlockSpec(memory_space=pltpu.VMEM), far],
        out_specs=far,
        scratch_shapes=[
            pltpu.VMEM(advanced.shape, jnp.float32),
            pltpu.VMEM(advanced.shape, jnp.bfloat16),
            pltpu.VMEM((steps, depth, columns * heads // 2), jnp.bfloat16),
            pltpu.VMEM(shape, jnp.bfloat16),
            pltpu.SemaphoreType.DMA((heads + 1,)),
            pltpu.SemaphoreType.DMA((heads // 4,)),
        ],
        compiler_params=pltpu.CompilerParams(vmem_limit_bytes=GRANT),
        cost_estimate=pl.CostEstimate(
            flops=6 * rows * width * heads * dim, bytes_accessed=10 * 2**20, transcendentals=0
        ),
    )(advanced, gain.reshape(1, -1), slices)


def mix_kernel(
    attended_ref, weight_ref, advanced_ref, copied_ref, mixed_ref,
    weight, advanced, mixed, done, sent,
):
    rows, width = advanced.shape
    chunks = weight.shape[0]
    wide = width // chunks
    load_advanced = pltpu.make_async_copy(advanced_ref, advanced, done.at[chunks + 1])
    loads = [
        pltpu.make_async_copy(weight_ref.at[:, b * wide : (b + 1) * wide], weight.at[b], done.at[b])
        for b in range(chunks)
    ]
    for load in (loads[0], load_advanced):
        load.start()
    token_rows = attended_ref[...].T
    for load in loads[1:]:
        load.start()
    stores = []
    for b in range(chunks):
        columns = slice(b * wide, (b + 1) * wide)
        loads[b].wait()
        product = jnp.dot(token_rows, weight[b], preferred_element_type=jnp.float32)
        if b == 0:
            load_advanced.wait()
            stores.append(pltpu.make_async_copy(advanced, copied_ref, sent.at[chunks]))
            stores[-1].start()
        mixed[:, columns] = advanced[:, columns] + product
        stores.append(
            pltpu.make_async_copy(mixed.at[:, columns], mixed_ref.at[:, columns], sent.at[b])
        )
        stores[-1].start()
    for store in stores:
        store.wait()


def mix(attended, weight, advanced):
    depth, rows = attended.shape
    width = advanced.shape[1]
    chunks = width // 256
    far = pl.BlockSpec(memory_space=pl.ANY)
    return pl.pallas_call(
        mix_kernel,
        out_shape=(jax.ShapeDtypeStruct(advanced.shape, jnp.float32),) * 2,
        in_specs=[pl.BlockSpec(memory_space=pltpu.VMEM), far, far],
        out_specs=(far, far),
        scratch_shapes=[
            pltpu.VMEM((chunks, depth, width // chunks), jnp.bfloat16),
            pltpu.VMEM(advanced.shape, jnp.float32),
            pltpu.VMEM(advanced.shape, jnp.float32),
            pltpu.SemaphoreType.DMA((chunks + 2,)),
            pltpu.SemaphoreType.DMA((chunks + 1,)),
        ],
        compiler_params=pltpu.CompilerParams(vmem_limit_bytes=48 * 2**20),
        cost_estimate=pl.CostEstimate(
            flops=2 * rows * depth * width, bytes_accessed=8 * 2**20, transcendentals=0
        ),
    )(attended, weight, advanced)


def swap(blocks, axis):
    return lax.all_to_all(blocks, axis, split_axis=0, concat_axis=0, tiled=True)


def local(states, start, noise, coefficients, context, qkv_weight, out_weights, gain):
    steps, seqs = lax.axis_size("step"), lax.axis_size("seq")
    step, seq = lax.axis_index("step"), lax.axis_index("seq")
    rows, width = start.shape
    tokens, dim = context.shape[1:]

    heads, chips = seqs, seqs // 2
    place = seq.astype(jnp.int32).reshape(1)
    pairs = [(i, i ^ 1) for i in range(seqs)]
    heads_tokens = context[0].T

    first_half, last_shard, *pieces = cut(
        place, heads_tokens, qkv_weight, out_weights, steps, chips
    )
    packed = swap(first_half, "step")

    pieces = [
        lax.ppermute(piece, "seq", [(i, (i + 2 * k + 2) % seqs) for i in range(seqs)])
        for k, piece in enumerate(pieces)
    ]
    kept, given, slices, mine = collect(place, heads_tokens, pieces, packed)
    slices = lax.all_gather(slices, "seq")
    taken = lax.ppermute(given, "seq", pairs)
    other = lax.ppermute(mine, "seq", pairs)
    drift = drift_of(place, coefficients[0], kept, taken, mine, other, states[0], noise[0])

    piece = rows // steps
    drifts = swap(drift.reshape(steps, piece, width), "step")
    advanced = sum_before(drifts, lax.dynamic_slice_in_dim(start, step * piece, piece, 0))
    advanced = swap(advanced, "step").reshape(rows, width)
    by_head = swap(project_qkv(advanced, gain, slices, qkv_weight.shape[0], dim), "seq")
    last_weight = lax.all_gather(last_shard, "step", axis=0, tiled=True)
    attended = swap(attend(by_head), "seq").reshape(seqs * dim, rows)
    advanced, mixed = mix(attended, last_weight, advanced)
    return (advanced[None], mixed[None])


def solution(mesh):
    placed = (
        P("step", "seq", None),
        P("seq", None),
        P("step", "seq", None),
        P("step", None),
        P("step", None, "seq"),
        P("step", None),
        P(None, "step", None),
        P(),
    )
    return jax.shard_map(
        local,
        mesh=mesh,
        in_specs=placed,
        out_specs=(P("step", "seq", None), P("step", "seq", None)),
        check_vma=False,
    )
```
